32 devices in a mesh: parts: 2 (over x), node: 2 (over core), rank: 8 (over z, y).
Axes of the slice: x: 2, y: 2, z: 4, core: 2. Of those that a mesh axis runs over, the one named last changes fastest.
Arguments:
- grad_out: bfloat16 [4096, 3584], P(('parts', 'node', 'rank')), parts along dimension 0, may hold values from -6 to 6
- expert_ids: int32 [4096, 2], P(('parts', 'node', 'rank')), parts along dimension 0, may hold values from 0 to 3, all different within a row; in each aligned block of 128 rows (0 to 127, 128 to 255, ...) at most 96 rows name the same one
- scores: float32 [4096, 2], P(('parts', 'node', 'rank')), parts along dimension 0, may hold values from 0.05 to 0.95
- gate_weight: bfloat16 [16, 3584, 256], P(('node', 'rank')), may hold values from -0.09375 to 0.09375
- up_weight: bfloat16 [16, 3584, 256], P(('node', 'rank')), may hold values from -0.09375 to 0.09375
- down_weight: bfloat16 [16, 256, 3584], P(('node', 'rank')), may hold values from -0.1875 to 0.1875
- saved_gate: bfloat16 [32, 1536, 256], P(('parts', 'node', 'rank')), parts along dimension 0, may hold values from -6 to 6
- saved_up: bfloat16 [32, 1536, 256], P(('parts', 'node', 'rank')), parts along dimension 0, may hold values from -1.5 to 1.5
Outputs:
- grad_in: bfloat16 [4096, 3584], P(('parts', 'node', 'rank')), parts along dimension 0
- grad_logit: float32 [4096, 2], P(('parts', 'node', 'rank')), parts along dimension 0
The draws below stay inside these ranges and needn't reach their ends.
There are 2 independent parts, one for each index of `parts`. The reference program is written for one: setup_inputs(seed, part) draws one part's arguments, and reference() takes and returns one part's arrays. A program takes and returns all parts, laid end to end along the dimension named above; an argument that names none is the same for every part. Nothing has to cross between parts.
Inputs may be any that keep to these rules, and one draw needn't show every extreme that they name: `expert_ids`: within the 128 tokens of one device no expert is chosen more than 96 times, a bound that some block reaches; a token's 2 experts differ.
All inputs are finite; a program needn't handle non-finite values.
Results may differ from the reference program's by a relative error of at most 0.0065.
Values may be sent and summed in bfloat16 or wider, within the bound.
A program may use at most 128 MiB of HBM per device.

```python
import math
import jax
import jax.numpy as jnp
import numpy as np
from jax import lax

D = 3584
FF = 1024
TOPK = 2
SPLIT = 4
TOK_DEV = 128
TOKENS = 2048
EXPERTS = 4
CAP = 96
N_NODE = 2
N_RANK = 8


def block_levels(rng, shape, split, least, largest):
    gain, own = 1.0, jax.random.fold_in(rng, 6)
    for axis_at, shards_of in split:
        heights = jnp.exp(jax.random.uniform(jax.random.fold_in(own, axis_at), (shards_of,), jnp.float32, least / len(split), largest / len(split)))
        gain = gain * jnp.repeat(heights, shape[axis_at] // shards_of).reshape([-1 if axis == axis_at else 1 for axis in range(len(shape))])
    return gain


def shared_out(key, own, number, rows, number_of, top, bound, slope):
    order = jax.random.permutation(key, number_of)
    packed, ordinary = shares(number_of, rows * top, bound, slope, True), shares(number_of, rows * top, bound, slope, False)
    places = jnp.arange(number_of)

    def named(lengths, turn):
        used = int((lengths > 0).sum())
        fixed = max(1, used // 4)
        shifted = fixed + (places - fixed + turn * (used - fixed)) % max(1, number_of - fixed)
        return jnp.zeros((number_of,), jnp.int32).at[order[jnp.where(places < fixed, places, shifted)]].set(jnp.asarray(lengths, jnp.int32))

    lengths = jnp.where(number % 4 == 0, named(packed, number // 4), named(ordinary, number - number // 4 - 1))
    mixed = jax.random.permutation(jax.random.fold_in(own, 3), number_of)
    donor, sink = mixed[0:number_of // 2 * 2:2], mixed[1:number_of // 2 * 2:2]
    slack = jnp.minimum(lengths[donor] - 1, bound - lengths[sink]) // 2
    slack = jnp.where((donor == order[0]) | (sink == order[0]) | (lengths[sink] == 0), 0, jnp.maximum(slack, 0))
    shifted = jax.random.randint(jax.random.fold_in(own, 4), (number_of // 2,), 0, 1 << 20) % (slack + 1)
    lengths = lengths.at[donor].add(-shifted).at[sink].add(shifted)
    members = jnp.searchsorted(jnp.cumsum(lengths), jnp.arange(rows * top), side="right").astype(jnp.int32)
    table = members.reshape(top, rows).T
    table = table[jax.random.permutation(jax.random.fold_in(own, 1), rows)]
    turn = jax.random.randint(jax.random.fold_in(own, 2), (rows, 1), 0, top)
    return jnp.take_along_axis(table, (jnp.arange(top)[None, :] + turn) % top, axis=1)


def shares(count, total, limit, skew, full):
    loads = [(1 << 20) // math.isqrt(rank ** skew) + 1 for rank in range(1, count + 1)]
    largest = limit if full else min(limit, max(-(-total // count), total * loads[0] // sum(loads)))
    least = 1 if total - largest >= count - 1 else 0
    given, spare = [largest] + [least] * (count - 1), total - largest - least * (count - 1)
    while spare > 0:
        movable = [i for i in range(1, count) if given[i] < largest] or [i for i in range(1, count) if given[i] < limit]
        pool, left = sum([loads[i] for i in movable]), spare
        for i in movable:
            extra = min(limit - given[i], max(1, left * loads[i] // pool), spare)
            given[i] = given[i] + extra
            spare = spare - extra
    return np.array(given)


def normal_values(stream_key, shape, spread, most, shards=(), held_as=jnp.bfloat16):
    array = jax.random.normal(stream_key, shape, jnp.float32) * spread
    if len(shards) > 0:
        array = block_levels(stream_key, shape, shards, -0.22, 0.18) * array
    return jnp.clip(array, min=-most, max=most).astype(held_as)


def setup_inputs(seed: int = 0, part: int = 0) -> dict:
    key_list = jax.random.split(jax.random.key(seed), 9)
    part_splits = jax.random.split(jax.random.fold_in(key_list[8], part), 9)
    grad_out = normal_values(part_splits[0], (TOKENS, D), 1.0, 6.0, ((0, 16),))
    expert_ids_keys = jax.random.split(jax.random.fold_in(part_splits[1], 1), TOKENS // TOK_DEV)
    expert_ids_turns = jax.random.permutation(jax.random.fold_in(part_splits[1], 3), TOKENS // TOK_DEV)
    expert_ids = jax.vmap(lambda own, number: shared_out(jax.random.fold_in(part_splits[1], 2), own, number, TOK_DEV, EXPERTS, TOPK, CAP, 2))(expert_ids_keys, expert_ids_turns).reshape((TOKENS, TOPK))
    scores = jnp.clip(0.05 + 0.9 * jax.random.uniform(part_splits[2], (TOKENS, TOPK), jnp.float32) ** block_levels(part_splits[2], (TOKENS, TOPK), ((0, 16),), -0.2, 0.2), 0.05, 0.95)
    gate_weight = normal_values(key_list[3], (EXPERTS * SPLIT, D, FF // SPLIT), D ** -0.5, 0.09375, ((0, 16),))
    up_weight = normal_values(key_list[4], (EXPERTS * SPLIT, D, FF // SPLIT), D ** -0.5, 0.09375, ((0, 16),))
    down_weight = normal_values(key_list[5], (EXPERTS * SPLIT, FF // SPLIT, D), FF ** -0.5, 0.1875, ((0, 16),))
    saved_gate = normal_values(part_splits[6], (EXPERTS * SPLIT, N_NODE * N_RANK * CAP, FF // SPLIT), 1.0, 6.0, ((0, 16),))
    saved_up = normal_values(part_splits[7], (EXPERTS * SPLIT, N_NODE * N_RANK * CAP, FF // SPLIT), 0.25, 1.5, ((0, 16),))
    return dict(grad_out=grad_out, expert_ids=expert_ids, scores=scores, gate_weight=gate_weight, up_weight=up_weight, down_weight=down_weight, saved_gate=saved_gate, saved_up=saved_up)


route_scale = 2.5


def slot_numbers(expert_ids, source_count):
    grouped = expert_ids.reshape(source_count, -1)
    onehot = (grouped[:, :, None] == jnp.arange(EXPERTS, dtype=jnp.int32)[None, None, :]).astype(jnp.int32)
    earlier = jnp.cumsum(onehot, axis=1) - onehot
    return jnp.sum(earlier * onehot, axis=2).reshape(expert_ids.shape).astype(jnp.int32)


def reference(grad_out, expert_ids, scores, gate_weight, up_weight, down_weight, saved_gate, saved_up):
    source_count = N_NODE * N_RANK
    slot_rows = source_count * CAP
    slot_index = slot_numbers(expert_ids, source_count)
    source_of = (jnp.arange(TOKENS, dtype=jnp.int32) // TOK_DEV)[:, None]
    location = (expert_ids * slot_rows + source_of * CAP + slot_index).astype(jnp.int32).reshape(-1)
    repeated = jnp.repeat(grad_out, TOPK, axis=0)
    dispatched = jnp.zeros((EXPERTS * slot_rows, D), jnp.bfloat16).at[location].set(repeated)
    contract = (((1,), (1,)), ((), ()))

    def one_expert(expert):
        rows_in = lax.dynamic_slice_in_dim(dispatched, (expert * slot_rows).astype(jnp.int32), slot_rows, 0)
        accumulated = jnp.zeros((slot_rows, D), jnp.float32)
        product_sum = jnp.zeros((slot_rows,), jnp.float32)
        for quarter in range(SPLIT):
            block_id = (expert * SPLIT + quarter).astype(jnp.int32)
            w_gate = lax.dynamic_index_in_dim(gate_weight, block_id, 0, keepdims=False)
            w_up = lax.dynamic_index_in_dim(up_weight, block_id, 0, keepdims=False)
            w_down = lax.dynamic_index_in_dim(down_weight, block_id, 0, keepdims=False)
            gate_pre = lax.dynamic_index_in_dim(saved_gate, block_id, 0, keepdims=False).astype(jnp.float32)
            up_pre = lax.dynamic_index_in_dim(saved_up, block_id, 0, keepdims=False).astype(jnp.float32)
            d_hidden = lax.dot_general(rows_in, w_down, contract, preferred_element_type=jnp.float32)
            gate_sigmoid = jax.nn.sigmoid(gate_pre)
            gate_act = gate_pre * gate_sigmoid
            product_part = jnp.sum(d_hidden * gate_act * up_pre, axis=1).astype(jnp.bfloat16)
            d_gate = (d_hidden * up_pre * gate_sigmoid * (1.0 + gate_pre * (1.0 - gate_sigmoid))).astype(jnp.bfloat16)
            d_up = (d_hidden * gate_act).astype(jnp.bfloat16)
            partial_sum = lax.dot_general(d_gate, w_gate, contract, preferred_element_type=jnp.float32)
            partial_sum = partial_sum + lax.dot_general(d_up, w_up, contract, preferred_element_type=jnp.float32)
            partial_bf = lax.optimization_barrier(partial_sum.astype(jnp.bfloat16))
            accumulated = accumulated + partial_bf.astype(jnp.float32)
            product_sum = product_sum + lax.optimization_barrier(product_part).astype(jnp.float32)
        return accumulated.astype(jnp.bfloat16), product_sum.astype(jnp.bfloat16)

    contributions, products = lax.map(one_expert, jnp.arange(EXPERTS, dtype=jnp.int32))
    contributions = contributions.reshape(EXPERTS * slot_rows, D)
    products = products.reshape(-1)
    place_pairs = location.reshape(TOKENS, TOPK)
    score_total = jnp.sum(scores, axis=1, keepdims=True)
    weights = route_scale * scores / score_total
    grad_sum = jnp.zeros((TOKENS, D), jnp.float32)
    for choice_k in range(TOPK):
        grad_sum = grad_sum + weights[:, choice_k:choice_k + 1] * contributions[place_pairs[:, choice_k]].astype(jnp.float32)
    grad_in = grad_sum.astype(jnp.bfloat16)
    picked_products = products[location].reshape(TOKENS, TOPK).astype(jnp.float32)
    centred = picked_products - jnp.sum(picked_products * scores, axis=1, keepdims=True) / score_total
    grad_logit = route_scale / score_total * centred * scores * (1.0 - scores)
    return grad_in, grad_logit
```

```python
import jax
import jax.numpy as jnp
from jax import lax
from jax.sharding import PartitionSpec as P

SPLIT = 4


route_scale = 2.5


def from_partner(block, axis, distance):
    count = lax.axis_size(axis)
    route = []
    for low in range(count):
        high = low | 1 << distance
        if high != low and high < count:
            route += [(low, high), (high, low)]
    return lax.ppermute(block, axis, route)


def take_half(stacked, chosen, axis_number):
    return lax.dynamic_index_in_dim(stacked, chosen, axis_number, keepdims=False)


def on_device(
    grad_out, expert_ids, scores, gate_weight, up_weight, down_weight, saved_gate, saved_up
):
    token_count, feature_width = grad_out.shape
    top_count = expert_ids.shape[1]
    source_count = lax.axis_size("node") * lax.axis_size("rank")
    expert_count = source_count // SPLIT
    hidden_width = gate_weight.shape[2]
    capacity = saved_gate.shape[1] // source_count
    quarter = capacity // SPLIT
    holder = lax.axis_index("rank") % SPLIT
    flat_ids = expert_ids.reshape(-1)
    onehot = (flat_ids[:, None] == jnp.arange(expert_count, dtype=jnp.int32)[None, :]).astype(
        jnp.int32
    )
    slot_index = jnp.sum((jnp.cumsum(onehot, axis=0) - onehot) * onehot, axis=1)
    slot_block = slot_index // quarter
    slot_within = slot_index % quarter
    repeated = jnp.repeat(grad_out, top_count, axis=0)
    empty_rows = jnp.zeros((expert_count * capacity, feature_width), jnp.bfloat16)
    location = (slot_block * expert_count + flat_ids) * quarter + slot_within
    buffered = (
        empty_rows.at[location]
        .set(repeated)
        .reshape(SPLIT, expert_count, 1, quarter, feature_width)
    )
    outgoing = jnp.broadcast_to(buffered, (SPLIT, expert_count, SPLIT, quarter, feature_width))
    outgoing = outgoing.reshape(SPLIT, source_count, quarter, feature_width)
    arrived = lax.all_to_all(outgoing, ("node", "rank"), split_axis=1, concat_axis=1, tiled=True)
    flat_rows = arrived.reshape(-1, feature_width)

    def arranged(saved):
        ordered = saved[0].reshape(source_count, SPLIT, quarter, hidden_width).transpose(1, 0, 2, 3)
        return ordered.reshape(-1, hidden_width).astype(jnp.float32)

    gate_pre = arranged(saved_gate)
    up_pre = arranged(saved_up)
    contract = (((1,), (1,)), ((), ()))
    d_hidden = lax.dot_general(
        flat_rows, down_weight[0], contract, preferred_element_type=jnp.float32
    )
    gate_sigmoid = jax.nn.sigmoid(gate_pre)
    gate_act = gate_pre * gate_sigmoid
    product_part = jnp.sum(d_hidden * gate_act * up_pre, axis=1).astype(jnp.bfloat16)
    d_gate = (d_hidden * up_pre * gate_sigmoid * (1.0 + gate_pre * (1.0 - gate_sigmoid))).astype(
        jnp.bfloat16
    )
    d_up = (d_hidden * gate_act).astype(jnp.bfloat16)
    partial_sum = lax.dot_general(
        d_gate, gate_weight[0], contract, preferred_element_type=jnp.float32
    )
    partial_sum = partial_sum + lax.dot_general(
        d_up, up_weight[0], contract, preferred_element_type=jnp.float32
    )
    partial_rows = partial_sum.astype(jnp.bfloat16).reshape(
        2, 2, source_count, quarter, feature_width
    )
    partial_products = product_part.reshape(2, 2, source_count, quarter)
    low_bit = holder % 2
    high_bit = holder // 2
    kept_rows = take_half(partial_rows, low_bit, 1)
    sent_rows = take_half(partial_rows, 1 - low_bit, 1)
    kept_products = take_half(partial_products, low_bit, 1)
    sent_products = take_half(partial_products, 1 - low_bit, 1)
    came_rows, came_products = from_partner((sent_rows, sent_products), "rank", 0)
    pair_rows = kept_rows.astype(jnp.float32) + came_rows.astype(jnp.float32)
    pair_products = kept_products.astype(jnp.float32) + came_products.astype(jnp.float32)
    kept_pair = take_half(pair_rows, high_bit, 0)
    sent_pair = take_half(pair_rows, 1 - high_bit, 0)
    kept_pair_products = take_half(pair_products, high_bit, 0)
    sent_pair_products = take_half(pair_products, 1 - high_bit, 0)
    came_pair, came_pair_products = from_partner((sent_pair, sent_pair_products), "rank", 1)
    summed_rows = (kept_pair + came_pair).astype(jnp.bfloat16)
    summed_products = (kept_pair_products + came_pair_products).astype(jnp.bfloat16)
    returned_rows, returned_products = (
        lax.all_to_all(summed_rows, ("node", "rank"), split_axis=0, concat_axis=0, tiled=True),
        lax.all_to_all(summed_products, ("node", "rank"), split_axis=0, concat_axis=0, tiled=True),
    )
    returned_rows = returned_rows.reshape(expert_count * capacity, feature_width)
    returned_products = returned_products.reshape(-1)
    gathered_at = flat_ids * capacity + slot_index
    picked = (
        returned_rows[gathered_at]
        .reshape(token_count, top_count, feature_width)
        .astype(jnp.float32)
    )
    picked_products = (
        returned_products[gathered_at].reshape(token_count, top_count).astype(jnp.float32)
    )
    score_total = jnp.sum(scores, axis=1, keepdims=True)
    weights = route_scale * scores / score_total
    grad_in = jnp.sum(weights[:, :, None] * picked, axis=1).astype(jnp.bfloat16)
    centred = (
        picked_products - jnp.sum(picked_products * scores, axis=1, keepdims=True) / score_total
    )
    grad_logit = route_scale / score_total * centred * scores * (1.0 - scores)
    return (grad_in, grad_logit)


def token_order(ids, scores, expert, capacity):
    lead = ids.shape[0]
    mine = jnp.any(ids == expert, axis=-1)
    slots = jnp.cumsum(mine.astype(jnp.int32), axis=1) - 1
    slots = jnp.where(mine, slots, -1)
    total = jnp.sum(scores, axis=-1)
    weight = jnp.sum(jnp.where(ids == expert, scores, 0.0), axis=-1) * route_scale / total
    pick = (slots[:, :, None] == jnp.arange(capacity)[None, None, :]).astype(jnp.bfloat16)
    return pick, weight


def dense_on_device(
    grad_out, expert_ids, scores, gate_weight, up_weight, down_weight, saved_gate, saved_up
):
    axes = ("node", "rank")
    token_count, feature_width = grad_out.shape
    source_count = lax.axis_size("node") * lax.axis_size("rank")
    expert_count = source_count // SPLIT
    hidden = gate_weight.shape[2]
    capacity = saved_gate.shape[1] // source_count
    expert = lax.axis_index(axes) // SPLIT
    rows = lax.all_gather(grad_out, axes, axis=0, tiled=True)
    ids = lax.all_gather(expert_ids, axes, axis=0, tiled=False)
    all_scores = lax.all_gather(scores, axes, axis=0, tiled=False)
    pick, weight = token_order(ids, all_scores, expert, capacity)

    def spread(saved):
        by_source = saved[0].reshape(source_count, capacity, hidden)
        return jnp.einsum("stc,sch->sth", pick, by_source, preferred_element_type=jnp.float32).reshape(-1, hidden)

    g = spread(saved_gate)
    u = spread(saved_up)
    contract = (((1,), (1,)), ((), ()))
    d_hidden = lax.dot_general(rows, down_weight[0], contract, preferred_element_type=jnp.float32)
    sig = jax.nn.sigmoid(g)
    act = g * sig
    part = jnp.sum(d_hidden * act * u, axis=1)
    scaled = d_hidden * weight.reshape(-1, 1)
    d_gate = (scaled * u * sig * (1.0 + g * (1.0 - sig))).astype(jnp.bfloat16)
    d_up = (scaled * act).astype(jnp.bfloat16)
    both = jnp.concatenate([d_gate, d_up], axis=1)
    weights = jnp.concatenate([gate_weight[0], up_weight[0]], axis=1)
    partial = lax.dot_general(both, weights, contract, preferred_element_type=jnp.float32)
    grad_in = lax.psum_scatter(partial.astype(jnp.bfloat16), axes, scatter_dimension=0, tiled=True)
    lanes = jnp.where(jnp.arange(expert_count)[None, :] == expert, part[:, None], 0.0)
    products = lax.psum_scatter(lanes, axes, scatter_dimension=0, tiled=True)
    picked = jnp.sum(jnp.where(expert_ids[:, :, None] == jnp.arange(expert_count)[None, None, :], products[:, None, :], 0.0), axis=2)
    total = jnp.sum(scores, axis=1, keepdims=True)
    centred = picked - jnp.sum(picked * scores, axis=1, keepdims=True) / total
    grad_logit = route_scale / total * centred * scores * (1.0 - scores)
    return grad_in, grad_logit


def solution(mesh):
    in_specs = (
        P(("parts", "node", "rank"), None),
        P(("parts", "node", "rank"), None),
        P(("parts", "node", "rank"), None),
        P(("node", "rank"), None, None),
        P(("node", "rank"), None, None),
        P(("node", "rank"), None, None),
        P(("parts", "node", "rank"), None, None),
        P(("parts", "node", "rank"), None, None),
    )
    out_specs = (P(("parts", "node", "rank"), None), P(("parts", "node", "rank"), None))
    few = mesh.shape["node"] * mesh.shape["rank"] <= 16
    return jax.shard_map(
        dense_on_device if few else on_device, mesh=mesh, in_specs=in_specs, out_specs=out_specs, check_vma=False
    )
```

```python
import jax
import jax.numpy as jnp
from jax import lax
from jax.experimental import pallas as pl
from jax.experimental.pallas import tpu as pltpu
from jax.sharding import PartitionSpec as P

SPLIT = 4


route_scale = 2.5


def from_partner(block, axis, distance):
    count = lax.axis_size(axis)
    route = []
    for low in range(count):
        high = low | 1 << distance
        if high != low and high < count:
            route += [(low, high), (high, low)]
    return lax.ppermute(block, axis, route)


def take_half(stacked, chosen, axis_number):
    return lax.dynamic_index_in_dim(stacked, chosen, axis_number, keepdims=False)


def on_device(
    grad_out, expert_ids, scores, gate_weight, up_weight, down_weight, saved_gate, saved_up
):
    token_count, feature_width = grad_out.shape
    top_count = expert_ids.shape[1]
    source_count = lax.axis_size("node") * lax.axis_size("rank")
    expert_count = source_count // SPLIT
    hidden_width = gate_weight.shape[2]
    capacity = saved_gate.shape[1] // source_count
    quarter = capacity // SPLIT
    holder = lax.axis_index("rank") % SPLIT
    flat_ids = expert_ids.reshape(-1)
    onehot = (flat_ids[:, None] == jnp.arange(expert_count, dtype=jnp.int32)[None, :]).astype(
        jnp.int32
    )
    slot_index = jnp.sum((jnp.cumsum(onehot, axis=0) - onehot) * onehot, axis=1)
    slot_block = slot_index // quarter
    slot_within = slot_index % quarter
    repeated = jnp.repeat(grad_out, top_count, axis=0)
    empty_rows = jnp.zeros((expert_count * capacity, feature_width), jnp.bfloat16)
    location = (slot_block * expert_count + flat_ids) * quarter + slot_within
    buffered = (
        empty_rows.at[location]
        .set(repeated)
        .reshape(SPLIT, expert_count, 1, quarter, feature_width)
    )
    outgoing = jnp.broadcast_to(buffered, (SPLIT, expert_count, SPLIT, quarter, feature_width))
    outgoing = outgoing.reshape(SPLIT, source_count, quarter, feature_width)
    arrived = lax.all_to_all(outgoing, ("node", "rank"), split_axis=1, concat_axis=1, tiled=True)
    flat_rows = arrived.reshape(-1, feature_width)

    def arranged(saved):
        ordered = saved[0].reshape(source_count, SPLIT, quarter, hidden_width).transpose(1, 0, 2, 3)
        return ordered.reshape(-1, hidden_width).astype(jnp.float32)

    gate_pre = arranged(saved_gate)
    up_pre = arranged(saved_up)
    contract = (((1,), (1,)), ((), ()))
    d_hidden = lax.dot_general(
        flat_rows, down_weight[0], contract, preferred_element_type=jnp.float32
    )
    gate_sigmoid = jax.nn.sigmoid(gate_pre)
    gate_act = gate_pre * gate_sigmoid
    product_part = jnp.sum(d_hidden * gate_act * up_pre, axis=1).astype(jnp.bfloat16)
    d_gate = (d_hidden * up_pre * gate_sigmoid * (1.0 + gate_pre * (1.0 - gate_sigmoid))).astype(
        jnp.bfloat16
    )
    d_up = (d_hidden * gate_act).astype(jnp.bfloat16)
    partial_sum = lax.dot_general(
        d_gate, gate_weight[0], contract, preferred_element_type=jnp.float32
    )
    partial_sum = partial_sum + lax.dot_general(
        d_up, up_weight[0], contract, preferred_element_type=jnp.float32
    )
    partial_rows = partial_sum.astype(jnp.bfloat16).reshape(
        2, 2, source_count, quarter, feature_width
    )
    partial_products = product_part.reshape(2, 2, source_count, quarter)
    low_bit = holder % 2
    high_bit = holder // 2
    kept_rows = take_half(partial_rows, low_bit, 1)
    sent_rows = take_half(partial_rows, 1 - low_bit, 1)
    kept_products = take_half(partial_products, low_bit, 1)
    sent_products = take_half(partial_products, 1 - low_bit, 1)
    came_rows, came_products = from_partner((sent_rows, sent_products), "rank", 0)
    pair_rows = kept_rows.astype(jnp.float32) + came_rows.astype(jnp.float32)
    pair_products = kept_products.astype(jnp.float32) + came_products.astype(jnp.float32)
    kept_pair = take_half(pair_rows, high_bit, 0)
    sent_pair = take_half(pair_rows, 1 - high_bit, 0)
    kept_pair_products = take_half(pair_products, high_bit, 0)
    sent_pair_products = take_half(pair_products, 1 - high_bit, 0)
    came_pair, came_pair_products = from_partner((sent_pair, sent_pair_products), "rank", 1)
    summed_rows = (kept_pair + came_pair).astype(jnp.bfloat16)
    summed_products = (kept_pair_products + came_pair_products).astype(jnp.bfloat16)
    returned_rows, returned_products = (
        lax.all_to_all(summed_rows, ("node", "rank"), split_axis=0, concat_axis=0, tiled=True),
        lax.all_to_all(summed_products, ("node", "rank"), split_axis=0, concat_axis=0, tiled=True),
    )
    returned_rows = returned_rows.reshape(expert_count * capacity, feature_width)
    returned_products = returned_products.reshape(-1)
    gathered_at = flat_ids * capacity + slot_index
    picked = (
        returned_rows[gathered_at]
        .reshape(token_count, top_count, feature_width)
        .astype(jnp.float32)
    )
    picked_products = (
        returned_products[gathered_at].reshape(token_count, top_count).astype(jnp.float32)
    )
    score_total = jnp.sum(scores, axis=1, keepdims=True)
    weights = route_scale * scores / score_total
    grad_in = jnp.sum(weights[:, :, None] * picked, axis=1).astype(jnp.bfloat16)
    centred = (
        picked_products - jnp.sum(picked_products * scores, axis=1, keepdims=True) / score_total
    )
    grad_logit = route_scale / score_total * centred * scores * (1.0 - scores)
    return (grad_in, grad_logit)


MESH = pl.DeviceIdType.MESH
F32 = jnp.float32
BF16 = jnp.bfloat16
NT = (((1,), (1,)), ((), ()))
NN = (((1,), (0,)), ((), ()))
WIDE = 512
ZS = 4


def dot(a, b, how):
    return lax.dot_general(a, b, how, preferred_element_type=F32)


def fused(
    ids_ref, scores_ref, x_hbm, gate_hbm, up_hbm, down_hbm, sg_hbm, su_hbm,
    out_ref, prod_ref,
    X, WD, WG, WU, SG, SU, META, DGU, QF, SS, SR, UPIN, DNIN, UPOUT, DNOUT, FIN, PRS, PRR,
    loc_sem, y_send, y_recv, x_send, x_recv, ag_send, ag_recv, sib_send, sib_recv,
    meta_send, meta_recv, pr_send, pr_recv, cs_send, cs_recv, u_send, u_recv, d_send, d_recv,
):
    T, D = x_hbm.shape
    H = gate_hbm.shape[1]
    CAP = SG.shape[3]
    NK = D // WIDE
    x = lax.axis_index("parts")
    c = lax.axis_index("node")
    r = lax.axis_index("rank")
    z = r // 2
    y = r % 2
    me = z * 2 + c
    expert = c * 2 + z // 2

    sibling = (x, 1 - c, r)
    y_peer = (x, c, z * 2 + 1 - y)
    x_peer = (1 - x, c, r)
    above = (x, c, jnp.minimum(z + 1, ZS - 1) * 2 + y)
    below = (x, c, jnp.maximum(z - 1, 0) * 2 + y)

    def column(o):
        p = (me + o) % 8
        return (x, p % 2, (p // 2) * 2 + y)

    def remote(src, dst, send, recv, peer):
        return pltpu.make_async_remote_copy(
            src_ref=src, dst_ref=dst, send_sem=send, recv_sem=recv, device_id=peer, device_id_type=MESH
        )

    barrier = pltpu.get_barrier_semaphore()
    for peer in [y_peer, x_peer] + [column(o) for o in range(1, 8)]:
        pl.semaphore_signal(barrier, inc=1, device_id=peer, device_id_type=MESH)
    pl.semaphore_wait(barrier, 9)

    def chunk(zz):
        return X.at[zz, pl.ds(pl.multiple_of(c * T, T), T)]

    def chunk_other(zz):
        return X.at[zz, pl.ds(pl.multiple_of((1 - c) * T, T), T)]

    def up_copy(d, src):
        return remote(src, chunk(z - d), ag_send.at[0, d], ag_recv.at[0, d], above)

    def down_copy(d, src):
        return remote(src, chunk(z + d), ag_send.at[1, d], ag_recv.at[1, d], below)

    def up_arrival(d):
        return remote(chunk(z - d), chunk(z - d), ag_send.at[0, d - 1], ag_recv.at[0, d - 1], below)

    def down_arrival(d):
        return remote(chunk(z + d), chunk(z + d), ag_send.at[1, d - 1], ag_recv.at[1, d - 1], above)

    def sib_copy(n, zz, src):
        return remote(src, chunk(zz), sib_send.at[n], sib_recv.at[n], sibling)

    def sib_arrival(n, zz):
        return remote(chunk_other(zz), chunk_other(zz), sib_send.at[n], sib_recv.at[n], sibling)

    @pl.when(z < ZS - 1)
    def _():
        up_copy(0, x_hbm).start()

    @pl.when(z > 0)
    def _():
        down_copy(0, x_hbm).start()

    def piece(n):
        if n == 0:
            half = pl.ds(pl.multiple_of(x * (H // 2), H // 2), H // 2)
            return down_hbm.at[half], WD.at[1, half]
        if n == 1:
            return sg_hbm.at[:, :, 1 - y], SG.at[1]
        return su_hbm.at[:, :, 1 - y], SU.at[1]

    def y_copy(n):
        src, dst = piece(n)
        return remote(src, dst, y_send.at[n], y_recv.at[n], y_peer)

    def y_arrival(n):
        dst = piece(n)[1]
        return remote(dst, dst, y_send.at[n], y_recv.at[n], y_peer)

    def rows_of(k, which):
        return pl.ds(pl.multiple_of(k * WIDE + which * (WIDE // 2), WIDE // 2), WIDE // 2)

    def gu_copies(k):
        rows = rows_of(k, x)
        return [
            remote(gate_hbm.at[rows], WG.at[1, rows], y_send.at[3 + k], y_recv.at[3 + k], y_peer),
            remote(up_hbm.at[rows], WU.at[1, rows], y_send.at[3 + NK + k], y_recv.at[3 + NK + k], y_peer),
        ]

    def gu_arrivals(k):
        rows = rows_of(k, x)
        return [
            remote(WG.at[1, rows], WG.at[1, rows], y_send.at[3 + k], y_recv.at[3 + k], y_peer),
            remote(WU.at[1, rows], WU.at[1, rows], y_send.at[3 + NK + k], y_recv.at[3 + NK + k], y_peer),
        ]

    def gu_across(k, which):
        rows = rows_of(k, which)
        return [
            remote(WG.at[1, rows], WG.at[1, rows], x_send.at[1 + k], x_recv.at[1 + k], x_peer),
            remote(WU.at[1, rows], WU.at[1, rows], x_send.at[1 + NK + k], x_recv.at[1 + NK + k], x_peer),
        ]

    def down_across(which):
        half = pl.ds(pl.multiple_of(which * (H // 2), H // 2), H // 2)
        return remote(WD.at[1, half], WD.at[1, half], x_send.at[0], x_recv.at[0], x_peer)

    for n in range(3):
        y_copy(n).start()

    def start_gu(k, _):
        for copy in gu_copies(k):
            copy.start()
        return 0

    lax.fori_loop(0, NK, start_gu, 0)

    sib_copy(0, z, x_hbm).start()
    local = [
        pltpu.make_async_copy(x_hbm, chunk(z), loc_sem.at[0]),
        pltpu.make_async_copy(down_hbm, WD.at[0], loc_sem.at[1]),
        pltpu.make_async_copy(gate_hbm, WG.at[0], loc_sem.at[2]),
        pltpu.make_async_copy(up_hbm, WU.at[0], loc_sem.at[3]),
        pltpu.make_async_copy(sg_hbm.at[:, :, y], SG.at[0], loc_sem.at[4]),
        pltpu.make_async_copy(su_hbm.at[:, :, y], SU.at[0], loc_sem.at[5]),
    ]
    for copy in local:
        copy.start()

    lane = lax.broadcasted_iota(jnp.int32, (T, T), 1)
    row = lax.broadcasted_iota(jnp.int32, (T, T), 0)
    ids = ids_ref[...]
    scores = scores_ref[...]
    hit0 = lane == ids[:, 0:1]
    hit1 = lane == ids[:, 1:2]
    hits = jnp.where(hit0 | hit1, 1.0, 0.0)
    earlier = jnp.where(lane < row, 1.0, 0.0).astype(BF16)
    slots = jnp.where(hits > 0.5, dot(earlier, hits.astype(BF16), NN), -1.0)
    factor = route_scale / (scores[:, 0:1] + scores[:, 1:2])
    weights = jnp.where(lane == ids[:, 0:1] + 4, factor * scores[:, 0:1], 0.0)
    weights = jnp.where(lane == ids[:, 1:2] + 4, factor * scores[:, 1:2], weights)
    META[0] = jnp.transpose(jnp.where(lane < 4, slots, weights))[0:8]
    for o in range(1, 8):
        remote(META.at[0], META.at[o], meta_send.at[o], meta_recv.at[o], column(o)).start()

    def take_up(d):
        @pl.when(z - d >= 0)
        def _():
            up_arrival(d).wait_recv()
            if d < ZS - 1:
                @pl.when(z + 1 <= ZS - 1)
                def _():
                    up_copy(d, chunk(z - d)).start()
            sib_copy(d, z - d, chunk(z - d)).start()

    def take_down(d):
        @pl.when(z + d <= ZS - 1)
        def _():
            down_arrival(d).wait_recv()
            if d < ZS - 1:
                @pl.when(z - 1 >= 0)
                def _():
                    down_copy(d, chunk(z + d)).start()
            sib_copy(3 + d, z + d, chunk(z + d)).start()

    def pass_gu(k):
        for copy in gu_arrivals(k):
            copy.wait_recv()
        for copy in gu_across(k, x):
            copy.start()

    take_up(1)
    take_down(1)
    y_arrival(0).wait_recv()
    down_across(x).start()
    take_up(2)
    take_down(2)
    ready = 4
    lax.fori_loop(0, ready, lambda k, _: (pass_gu(k), 0)[1], 0)
    take_up(3)
    take_down(3)
    for copy in local:
        copy.wait()
    y_arrival(1).wait_recv()
    y_arrival(2).wait_recv()
    down_across(1 - x).wait_recv()
    for o in range(1, 8):
        remote(META.at[o], META.at[o], meta_send.at[o], meta_recv.at[o], column(o)).wait_recv()
    sib_arrival(0, z).wait_recv()
    for d in range(1, ZS):
        @pl.when(z - d >= 0)
        def _():
            sib_arrival(d, z - d).wait_recv()

        @pl.when(z + d <= ZS - 1)
        def _():
            sib_arrival(3 + d, z + d).wait_recv()

    slot_lane = lax.broadcasted_iota(jnp.int32, (T, CAP), 1).astype(F32)
    row8 = lax.broadcasted_iota(jnp.int32, (8, T), 0)
    ones = jnp.ones((8, H), BF16)

    def hidden(zz, _):
        hs = [dot(X[zz], WD[b], NT) for b in range(2)]
        for cc in range(2):
            o = (me - (zz * 2 + cc) + 8) % 8
            meta = jnp.transpose(jnp.concatenate([META[o], jnp.zeros((T - 8, T), F32)], axis=0))
            slot = jnp.sum(jnp.where(lane == expert, meta, 0.0), axis=1, keepdims=True)
            weight = jnp.sum(jnp.where(lane == expert + 4, meta, 0.0), axis=1, keepdims=True)
            pick = jnp.where(slot == slot_lane, 1.0, 0.0).astype(BF16)
            total = jnp.zeros((8, T), F32)
            for b in range(2):
                h = hs[b][cc * T:(cc + 1) * T]
                g = dot(pick, SG[b, cc, zz], NN)
                u = dot(pick, SU[b, cc, zz], NN)
                sig = jax.nn.sigmoid(g)
                act = g * sig
                prod = h * act * u
                high = prod.astype(BF16)
                low = (prod - high.astype(F32)).astype(BF16)
                total = total + dot(ones, high, NT) + dot(ones, low, NT)
                scaled = h * weight
                rows = pl.ds(pl.multiple_of(zz * T, T), T)
                DGU[cc, rows, b * 2 * H:b * 2 * H + H] = (
                    scaled * u * sig * (1.0 + g * (1.0 - sig))
                ).astype(BF16)
                DGU[cc, rows, b * 2 * H + H:(b + 1) * 2 * H] = (scaled * act).astype(BF16)
            PRS[zz * 2 + cc] = jnp.where(row8 == expert, total, 0.0)
        return 0

    lax.fori_loop(0, ZS, hidden, 0)
    for o in range(1, 8):
        remote(PRS.at[(me + o) % 8], PRR.at[o], pr_send.at[o], pr_recv.at[o], column(o)).start()

    def share(k):
        return remote(SS.at[k], SR.at[k], cs_send.at[k], cs_recv.at[k], sibling)

    def up_out(k, d):
        return remote(UPOUT.at[d - 1, k], UPIN.at[d - 1, k], u_send.at[d - 1, k], u_recv.at[d - 1, k], above)

    def down_out(k, d):
        return remote(DNOUT.at[d - 1, k], DNIN.at[d - 1, k], d_send.at[d - 1, k], d_recv.at[d - 1, k], below)

    def up_in(k, d):
        return remote(UPIN.at[d, k], UPIN.at[d, k], u_send.at[d, k], u_recv.at[d, k], below)

    def down_in(k, d):
        return remote(DNIN.at[d, k], DNIN.at[d, k], d_send.at[d, k], d_recv.at[d, k], above)

    def partial(k, cc):
        rows = pl.ds(pl.multiple_of(k * WIDE, WIDE), WIDE)
        acc = dot(DGU[cc, :, 0:H], WG[0, rows], NT)
        acc = acc + dot(DGU[cc, :, H:2 * H], WU[0, rows], NT)
        acc = acc + dot(DGU[cc, :, 2 * H:3 * H], WG[1, rows], NT)
        return acc + dot(DGU[cc, :, 3 * H:4 * H], WU[1, rows], NT)

    def compute(k):
        for copy in gu_across(k, 1 - x):
            copy.wait_recv()
        SS[k] = partial(k, 1 - c).reshape(ZS, T, WIDE).astype(BF16)
        share(k).start()
        QF[k % 4] = partial(k, c).reshape(ZS, T, WIDE)

    def mine(k, zz):
        return QF[k % 4, zz] + SR[k, zz].astype(F32)

    def chain(k):
        share(k).wait_recv()
        for d in (3, 2, 1):
            @pl.when(z + d <= ZS - 1)
            def _():
                @pl.when(z == 0)
                def _():
                    UPOUT[d - 1, k] = mine(k, z + d).astype(BF16)
                if d < 3:
                    @pl.when(z > 0)
                    def _():
                        up_in(k, d).wait_recv()
                        UPOUT[d - 1, k] = (mine(k, z + d) + UPIN[d, k].astype(F32)).astype(BF16)
                up_out(k, d).start()

            @pl.when(z - d >= 0)
            def _():
                @pl.when(z == ZS - 1)
                def _():
                    DNOUT[d - 1, k] = mine(k, z - d).astype(BF16)
                if d < 3:
                    @pl.when(z < ZS - 1)
                    def _():
                        down_in(k, d).wait_recv()
                        DNOUT[d - 1, k] = (mine(k, z - d) + DNIN[d, k].astype(F32)).astype(BF16)
                down_out(k, d).start()

    def final(k):
        FIN[...] = mine(k, z)

        @pl.when(z > 0)
        def _():
            up_in(k, 0).wait_recv()
            FIN[...] += UPIN[0, k].astype(F32)

        @pl.when(z < ZS - 1)
        def _():
            down_in(k, 0).wait_recv()
            FIN[...] += DNIN[0, k].astype(F32)

        out_ref[:, pl.ds(pl.multiple_of(k * WIDE, WIDE), WIDE)] = FIN[...].astype(BF16)

    def step(i, _):
        @pl.when(i + ready < NK)
        def _():
            pass_gu(i + ready)

        @pl.when(i < NK)
        def _():
            compute(i)

        @pl.when((i >= 1) & (i <= NK))
        def _():
            chain(i - 1)

        @pl.when(i >= 2)
        def _():
            final(i - 2)

        return 0

    lax.fori_loop(0, NK + 2, step, 0)

    total = PRS[me]
    for o in range(1, 8):
        remote(PRR.at[o], PRR.at[o], pr_send.at[o], pr_recv.at[o], column(o)).wait_recv()
        total = total + PRR[o]
    prod_ref[...] = total

    for o in range(1, 8):
        remote(META.at[0], META.at[o], meta_send.at[o], meta_recv.at[o], column(o)).wait_send()
        remote(PRS.at[(me + o) % 8], PRR.at[o], pr_send.at[o], pr_recv.at[o], column(o)).wait_send()
    for n in range(3):
        y_copy(n).wait_send()
    down_across(x).wait_send()
    sib_copy(0, z, x_hbm).wait_send()

    @pl.when(z < ZS - 1)
    def _():
        up_copy(0, x_hbm).wait_send()

    @pl.when(z > 0)
    def _():
        down_copy(0, x_hbm).wait_send()

    for d in range(1, ZS):
        @pl.when(z - d >= 0)
        def _():
            sib_copy(d, z - d, chunk(z - d)).wait_send()
            if d < ZS - 1:
                @pl.when(z + 1 <= ZS - 1)
                def _():
                    up_copy(d, chunk(z - d)).wait_send()

        @pl.when(z + d <= ZS - 1)
        def _():
            sib_copy(3 + d, z + d, chunk(z + d)).wait_send()
            if d < ZS - 1:
                @pl.when(z - 1 >= 0)
                def _():
                    down_copy(d, chunk(z + d)).wait_send()

    def finish(k, _):
        for copy in gu_copies(k) + gu_across(k, x):
            copy.wait_send()
        share(k).wait_send()
        for d in (3, 2, 1):
            @pl.when(z + d <= ZS - 1)
            def _():
                up_out(k, d).wait_send()

            @pl.when(z - d >= 0)
            def _():
                down_out(k, d).wait_send()
        return 0

    lax.fori_loop(0, NK, finish, 0)


def fused_on_device(
    grad_out, expert_ids, scores, gate_weight, up_weight, down_weight, saved_gate, saved_up
):
    T, D = grad_out.shape
    H = gate_weight.shape[2]
    cap = saved_gate.shape[1] // 16
    NK = D // WIDE
    dma = pltpu.SemaphoreType.DMA
    vmem = pl.BlockSpec(memory_space=pltpu.VMEM)
    hbm = pl.BlockSpec(memory_space=pl.ANY)
    grad_in, products = pl.pallas_call(
        fused,
        out_shape=(jax.ShapeDtypeStruct((T, D), BF16), jax.ShapeDtypeStruct((8, T), F32)),
        in_specs=[vmem, vmem] + [hbm] * 6,
        out_specs=(vmem, vmem),
        scratch_shapes=[
            pltpu.VMEM((ZS, 2 * T, D), BF16),
            pltpu.VMEM((2, H, D), BF16),
            pltpu.VMEM((2, D, H), BF16),
            pltpu.VMEM((2, D, H), BF16),
            pltpu.VMEM((2, 2, ZS, cap, H), BF16),
            pltpu.VMEM((2, 2, ZS, cap, H), BF16),
            pltpu.VMEM((8, 8, T), F32),
            pltpu.VMEM((2, ZS * T, 4 * H), BF16),
            pltpu.VMEM((4, ZS, T, WIDE), F32),
            pltpu.VMEM((NK, ZS, T, WIDE), BF16),
            pltpu.VMEM((NK, ZS, T, WIDE), BF16),
            pltpu.VMEM((3, NK, T, WIDE), BF16),
            pltpu.VMEM((3, NK, T, WIDE), BF16),
            pltpu.VMEM((3, NK, T, WIDE), BF16),
            pltpu.VMEM((3, NK, T, WIDE), BF16),
            pltpu.VMEM((T, WIDE), F32),
            pltpu.VMEM((8, 8, T), F32),
            pltpu.VMEM((8, 8, T), F32),
            dma((6,)),
            dma((3 + 2 * NK,)), dma((3 + 2 * NK,)),
            dma((1 + 2 * NK,)), dma((1 + 2 * NK,)),
            dma((2, 3)), dma((2, 3)),
            dma((7,)), dma((7,)),
            dma((8,)), dma((8,)),
            dma((8,)), dma((8,)),
            dma((NK,)), dma((NK,)),
            dma((3, NK)), dma((3, NK)),
            dma((3, NK)), dma((3, NK)),
        ],
        compiler_params=pltpu.CompilerParams(
            collective_id=0, has_side_effects=True, vmem_limit_bytes=62 * 1024 * 1024
        ),
    )(
        expert_ids, scores, grad_out, gate_weight[0], up_weight[0], down_weight[0],
        saved_gate.reshape(2, ZS, 2, cap, H), saved_up.reshape(2, ZS, 2, cap, H),
    )
    hit = expert_ids[:, :, None] == jnp.arange(8, dtype=jnp.int32)[None, None, :]
    picked = jnp.sum(jnp.where(hit, products.T[:, None, :], 0.0), axis=2)
    total = jnp.sum(scores, axis=1, keepdims=True)
    centred = picked - jnp.sum(picked * scores, axis=1, keepdims=True) / total
    grad_logit = route_scale / total * centred * scores * (1.0 - scores)
    return grad_in, grad_logit


def solution(mesh):
    in_specs = (
        P(("parts", "node", "rank"), None),
        P(("parts", "node", "rank"), None),
        P(("parts", "node", "rank"), None),
        P(("node", "rank"), None, None),
        P(("node", "rank"), None, None),
        P(("node", "rank"), None, None),
        P(("parts", "node", "rank"), None, None),
        P(("parts", "node", "rank"), None, None),
    )
    out_specs = (P(("parts", "node", "rank"), None), P(("parts", "node", "rank"), None))
    small = (mesh.shape["parts"], mesh.shape["node"], mesh.shape["rank"]) == (2, 2, 8)
    return jax.shard_map(
        fused_on_device if small else on_device, mesh=mesh, in_specs=in_specs, out_specs=out_specs, check_vma=False
    )
```

```python
import jax
import jax.numpy as jnp
from jax import lax
from jax.experimental import pallas as pl
from jax.experimental.pallas import tpu as pltpu
from jax.sharding import PartitionSpec as P

SPLIT = 4


route_scale = 2.5


def from_partner(block, axis, distance):
    count = lax.axis_size(axis)
    route = []
    for low in range(count):
        high = low | 1 << distance
        if high != low and high < count:
            route += [(low, high), (high, low)]
    return lax.ppermute(block, axis, route)


def take_half(stacked, chosen, axis_number):
    return lax.dynamic_index_in_dim(stacked, chosen, axis_number, keepdims=False)


def on_device(
    grad_out, expert_ids, scores, gate_weight, up_weight, down_weight, saved_gate, saved_up
):
    token_count, feature_width = grad_out.shape
    top_count = expert_ids.shape[1]
    source_count = lax.axis_size("node") * lax.axis_size("rank")
    expert_count = source_count // SPLIT
    hidden_width = gate_weight.shape[2]
    capacity = saved_gate.shape[1] // source_count
    quarter = capacity // SPLIT
    holder = lax.axis_index("rank") % SPLIT
    flat_ids = expert_ids.reshape(-1)
    onehot = (flat_ids[:, None] == jnp.arange(expert_count, dtype=jnp.int32)[None, :]).astype(
        jnp.int32
    )
    slot_index = jnp.sum((jnp.cumsum(onehot, axis=0) - onehot) * onehot, axis=1)
    slot_block = slot_index // quarter
    slot_within = slot_index % quarter
    repeated = jnp.repeat(grad_out, top_count, axis=0)
    empty_rows = jnp.zeros((expert_count * capacity, feature_width), jnp.bfloat16)
    location = (slot_block * expert_count + flat_ids) * quarter + slot_within
    buffered = (
        empty_rows.at[location]
        .set(repeated)
        .reshape(SPLIT, expert_count, 1, quarter, feature_width)
    )
    outgoing = jnp.broadcast_to(buffered, (SPLIT, expert_count, SPLIT, quarter, feature_width))
    outgoing = outgoing.reshape(SPLIT, source_count, quarter, feature_width)
    arrived = lax.all_to_all(outgoing, ("node", "rank"), split_axis=1, concat_axis=1, tiled=True)
    flat_rows = arrived.reshape(-1, feature_width)

    def arranged(saved):
        ordered = saved[0].reshape(source_count, SPLIT, quarter, hidden_width).transpose(1, 0, 2, 3)
        return ordered.reshape(-1, hidden_width).astype(jnp.float32)

    gate_pre = arranged(saved_gate)
    up_pre = arranged(saved_up)
    contract = (((1,), (1,)), ((), ()))
    d_hidden = lax.dot_general(
        flat_rows, down_weight[0], contract, preferred_element_type=jnp.float32
    )
    gate_sigmoid = jax.nn.sigmoid(gate_pre)
    gate_act = gate_pre * gate_sigmoid
    product_part = jnp.sum(d_hidden * gate_act * up_pre, axis=1).astype(jnp.bfloat16)
    d_gate = (d_hidden * up_pre * gate_sigmoid * (1.0 + gate_pre * (1.0 - gate_sigmoid))).astype(
        jnp.bfloat16
    )
    d_up = (d_hidden * gate_act).astype(jnp.bfloat16)
    partial_sum = lax.dot_general(
        d_gate, gate_weight[0], contract, preferred_element_type=jnp.float32
    )
    partial_sum = partial_sum + lax.dot_general(
        d_up, up_weight[0], contract, preferred_element_type=jnp.float32
    )
    partial_rows = partial_sum.astype(jnp.bfloat16).reshape(
        2, 2, source_count, quarter, feature_width
    )
    partial_products = product_part.reshape(2, 2, source_count, quarter)
    low_bit = holder % 2
    high_bit = holder // 2
    kept_rows = take_half(partial_rows, low_bit, 1)
    sent_rows = take_half(partial_rows, 1 - low_bit, 1)
    kept_products = take_half(partial_products, low_bit, 1)
    sent_products = take_half(partial_products, 1 - low_bit, 1)
    came_rows, came_products = from_partner((sent_rows, sent_products), "rank", 0)
    pair_rows = kept_rows.astype(jnp.float32) + came_rows.astype(jnp.float32)
    pair_products = kept_products.astype(jnp.float32) + came_products.astype(jnp.float32)
    kept_pair = take_half(pair_rows, high_bit, 0)
    sent_pair = take_half(pair_rows, 1 - high_bit, 0)
    kept_pair_products = take_half(pair_products, high_bit, 0)
    sent_pair_products = take_half(pair_products, 1 - high_bit, 0)
    came_pair, came_pair_products = from_partner((sent_pair, sent_pair_products), "rank", 1)
    summed_rows = (kept_pair + came_pair).astype(jnp.bfloat16)
    summed_products = (kept_pair_products + came_pair_products).astype(jnp.bfloat16)
    returned_rows, returned_products = (
        lax.all_to_all(summed_rows, ("node", "rank"), split_axis=0, concat_axis=0, tiled=True),
        lax.all_to_all(summed_products, ("node", "rank"), split_axis=0, concat_axis=0, tiled=True),
    )
    returned_rows = returned_rows.reshape(expert_count * capacity, feature_width)
    returned_products = returned_products.reshape(-1)
    gathered_at = flat_ids * capacity + slot_index
    picked = (
        returned_rows[gathered_at]
        .reshape(token_count, top_count, feature_width)
        .astype(jnp.float32)
    )
    picked_products = (
        returned_products[gathered_at].reshape(token_count, top_count).astype(jnp.float32)
    )
    score_total = jnp.sum(scores, axis=1, keepdims=True)
    weights = route_scale * scores / score_total
    grad_in = jnp.sum(weights[:, :, None] * picked, axis=1).astype(jnp.bfloat16)
    centred = (
        picked_products - jnp.sum(picked_products * scores, axis=1, keepdims=True) / score_total
    )
    grad_logit = route_scale / score_total * centred * scores * (1.0 - scores)
    return (grad_in, grad_logit)


MESH = pl.DeviceIdType.MESH
F32 = jnp.float32
BF16 = jnp.bfloat16
NT = (((1,), (1,)), ((), ()))
NN = (((1,), (0,)), ((), ()))
WIDE = 512
ZS = 4


def dot(a, b, how):
    return lax.dot_general(a, b, how, preferred_element_type=F32)


def fused(
    ids_ref, scores_ref, x_hbm, gate_hbm, up_hbm, down_hbm, sg_hbm, su_hbm,
    out_ref, prod_ref,
    X, WD, WG, WU, SG, SU, META, DGU, QF, SS, SR, UPIN, DNIN, UPOUT, DNOUT, FIN, PRS, PRR,
    loc_sem, y_send, y_recv, x_send, x_recv, ag_send, ag_recv, sib_send, sib_recv,
    meta_send, meta_recv, pr_send, pr_recv, cs_send, cs_recv, u_send, u_recv, d_send, d_recv,
):
    T, D = x_hbm.shape
    H = gate_hbm.shape[1]
    CAP = SG.shape[3]
    NK = D // WIDE
    x = lax.axis_index("parts")
    c = lax.axis_index("node")
    r = lax.axis_index("rank")
    z = r // 2
    y = r % 2
    me = z * 2 + c
    expert = c * 2 + z // 2

    sibling = (x, 1 - c, r)
    y_peer = (x, c, z * 2 + 1 - y)
    x_peer = (1 - x, c, r)
    above = (x, c, jnp.minimum(z + 1, ZS - 1) * 2 + y)
    below = (x, c, jnp.maximum(z - 1, 0) * 2 + y)

    def column(o):
        p = (me + o) % 8
        return (x, p % 2, (p // 2) * 2 + y)

    def remote(src, dst, send, recv, peer):
        return pltpu.make_async_remote_copy(
            src_ref=src, dst_ref=dst, send_sem=send, recv_sem=recv, device_id=peer, device_id_type=MESH
        )

    barrier = pltpu.get_barrier_semaphore()
    for peer in [y_peer, x_peer] + [column(o) for o in range(1, 8)]:
        pl.semaphore_signal(barrier, inc=1, device_id=peer, device_id_type=MESH)
    pl.semaphore_wait(barrier, 9)

    def chunk(zz):
        return X.at[zz, pl.ds(pl.multiple_of(c * T, T), T)]

    def chunk_other(zz):
        return X.at[zz, pl.ds(pl.multiple_of((1 - c) * T, T), T)]

    def up_copy(d, src):
        return remote(src, chunk(z - d), ag_send.at[0, d], ag_recv.at[0, d], above)

    def down_copy(d, src):
        return remote(src, chunk(z + d), ag_send.at[1, d], ag_recv.at[1, d], below)

    def up_arrival(d):
        return remote(chunk(z - d), chunk(z - d), ag_send.at[0, d - 1], ag_recv.at[0, d - 1], below)

    def down_arrival(d):
        return remote(chunk(z + d), chunk(z + d), ag_send.at[1, d - 1], ag_recv.at[1, d - 1], above)

    def sib_copy(n, zz, src):
        return remote(src, chunk(zz), sib_send.at[n], sib_recv.at[n], sibling)

    def sib_arrival(n, zz):
        return remote(chunk_other(zz), chunk_other(zz), sib_send.at[n], sib_recv.at[n], sibling)

    @pl.when(z < ZS - 1)
    def _():
        up_copy(0, x_hbm).start()

    @pl.when(z > 0)
    def _():
        down_copy(0, x_hbm).start()

    def job(s):
        order = ((1, 2, 3, 0), (0, 2, 3, 1), (3, 1, 0, 2), (2, 1, 0, 3))
        return jnp.where(
            z == 0, order[0][s], jnp.where(z == 1, order[1][s], jnp.where(z == 2, order[2][s], order[3][s]))
        )

    EIGHTH = H // 8

    def down_rows(n, which):
        return pl.ds(pl.multiple_of(which * (H // 2) + n * EIGHTH, EIGHTH), EIGHTH)

    def gu_rows(k, which):
        return pl.ds(pl.multiple_of(k * WIDE + which * (WIDE // 2), WIDE // 2), WIDE // 2)

    def refs_down(n, which):
        rows = down_rows(n, which)
        return [(down_hbm.at[rows], WD.at[1, rows], n)]

    def refs_gu(k, which):
        rows = gu_rows(k, which)
        return [(gate_hbm.at[rows], WG.at[1, rows], 4 + k), (up_hbm.at[rows], WU.at[1, rows], 4 + NK + k)]

    def refs_saved(s):
        zz = job(s)
        base = 4 + 2 * NK + 2 * s
        return [
            (sg_hbm.at[:, zz, 1 - y], SG.at[1, :, zz], base),
            (su_hbm.at[:, zz, 1 - y], SU.at[1, :, zz], base + 1),
        ]

    def over_y(refs):
        return [remote(src, dst, y_send.at[n], y_recv.at[n], y_peer) for src, dst, n in refs]

    def from_y(refs):
        return [remote(dst, dst, y_send.at[n], y_recv.at[n], y_peer) for _, dst, n in refs]

    def over_x(refs):
        return [remote(dst, dst, x_send.at[n], x_recv.at[n], x_peer) for _, dst, n in refs]

    def begin(copies):
        for copy in copies:
            copy.start()

    def arrive(copies):
        for copy in copies:
            copy.wait_recv()

    for n in range(4):
        begin(over_y(refs_down(n, x)))

    sib_copy(0, z, x_hbm).start()
    local = [
        pltpu.make_async_copy(x_hbm, chunk(z), loc_sem.at[0]),
        pltpu.make_async_copy(down_hbm, WD.at[0], loc_sem.at[1]),
        pltpu.make_async_copy(gate_hbm, WG.at[0], loc_sem.at[2]),
        pltpu.make_async_copy(up_hbm, WU.at[0], loc_sem.at[3]),
        pltpu.make_async_copy(sg_hbm.at[:, :, y], SG.at[0], loc_sem.at[4]),
        pltpu.make_async_copy(su_hbm.at[:, :, y], SU.at[0], loc_sem.at[5]),
    ]
    for copy in local:
        copy.start()

    lane = lax.broadcasted_iota(jnp.int32, (T, T), 1)
    row = lax.broadcasted_iota(jnp.int32, (T, T), 0)
    ids = ids_ref[...]
    scores = scores_ref[...]
    hit0 = lane == ids[:, 0:1]
    hit1 = lane == ids[:, 1:2]
    hits = jnp.where(hit0 | hit1, 1.0, 0.0)
    earlier = jnp.where(lane < row, 1.0, 0.0).astype(BF16)
    slots = jnp.where(hits > 0.5, dot(earlier, hits.astype(BF16), NN), -1.0)
    factor = route_scale / (scores[:, 0:1] + scores[:, 1:2])
    weights = jnp.where(lane == ids[:, 0:1] + 4, factor * scores[:, 0:1], 0.0)
    weights = jnp.where(lane == ids[:, 1:2] + 4, factor * scores[:, 1:2], weights)
    META[0] = jnp.transpose(jnp.where(lane < 4, slots, weights))[0:8]
    for o in range(1, 8):
        remote(META.at[0], META.at[o], meta_send.at[o], meta_recv.at[o], column(o)).start()

    def take_up(d):
        @pl.when(z - d >= 0)
        def _():
            up_arrival(d).wait_recv()
            if d < ZS - 1:
                @pl.when(z + 1 <= ZS - 1)
                def _():
                    up_copy(d, chunk(z - d)).start()
            sib_copy(d, z - d, chunk(z - d)).start()

    def take_down(d):
        @pl.when(z + d <= ZS - 1)
        def _():
            down_arrival(d).wait_recv()
            if d < ZS - 1:
                @pl.when(z - 1 >= 0)
                def _():
                    down_copy(d, chunk(z + d)).start()
            sib_copy(3 + d, z + d, chunk(z + d)).start()

    def pass_on(refs):
        arrive(from_y(refs))
        begin(over_x(refs))

    slot_lane = lax.broadcasted_iota(jnp.int32, (T, CAP), 1).astype(F32)
    row8 = lax.broadcasted_iota(jnp.int32, (8, T), 0)
    ones = jnp.ones((8, H), BF16)

    def hidden(s):
        zz = job(s)
        hs = [dot(X[zz], WD[b], NT) for b in range(2)]
        for cc in range(2):
            o = (me - (zz * 2 + cc) + 8) % 8
            meta = jnp.transpose(jnp.concatenate([META[o], jnp.zeros((T - 8, T), F32)], axis=0))
            slot = jnp.sum(jnp.where(lane == expert, meta, 0.0), axis=1, keepdims=True)
            weight = jnp.sum(jnp.where(lane == expert + 4, meta, 0.0), axis=1, keepdims=True)
            pick = jnp.where(slot == slot_lane, 1.0, 0.0).astype(BF16)
            total = jnp.zeros((8, T), F32)
            rows = pl.ds(pl.multiple_of(((cc + c) % 2) * T, T), T)
            for b in range(2):
                h = hs[b][cc * T:(cc + 1) * T]
                g = dot(pick, SG[b, cc, zz], NN)
                u = dot(pick, SU[b, cc, zz], NN)
                sig = jax.nn.sigmoid(g)
                act = g * sig
                prod = h * act * u
                high = prod.astype(BF16)
                low = (prod - high.astype(F32)).astype(BF16)
                total = total + dot(ones, high, NT) + dot(ones, low, NT)
                scaled = h * weight
                DGU[s, rows, b * 2 * H:b * 2 * H + H] = (
                    scaled * u * sig * (1.0 + g * (1.0 - sig))
                ).astype(BF16)
                DGU[s, rows, b * 2 * H + H:(b + 1) * 2 * H] = (scaled * act).astype(BF16)
            PRS[zz * 2 + cc] = jnp.where(row8 == expert, total, 0.0)

    def share(s, k):
        return remote(SS.at[s, k], SR.at[s, k], cs_send.at[s, k], cs_recv.at[s, k], sibling)

    def up_out(s, k):
        return remote(UPOUT.at[s, k], UPIN.at[s, k], u_send.at[s, k], u_recv.at[s, k], above)

    def down_out(s, k):
        return remote(DNOUT.at[s, k], DNIN.at[s, k], d_send.at[s, k], d_recv.at[s, k], below)

    def up_in(s, k):
        return remote(UPIN.at[s, k], UPIN.at[s, k], u_send.at[s, k], u_recv.at[s, k], below)

    def down_in(s, k):
        return remote(DNIN.at[s, k], DNIN.at[s, k], d_send.at[s, k], d_recv.at[s, k], above)

    def compute(s, k):
        rows = pl.ds(pl.multiple_of(k * WIDE, WIDE), WIDE)
        acc = dot(DGU[s, :, 0:H], WG[0, rows], NT)
        acc = acc + dot(DGU[s, :, H:2 * H], WU[0, rows], NT)
        acc = acc + dot(DGU[s, :, 2 * H:3 * H], WG[1, rows], NT)
        acc = acc + dot(DGU[s, :, 3 * H:4 * H], WU[1, rows], NT)
        SS[s, k] = acc[T:2 * T].astype(BF16)
        share(s, k).start()
        QF[s, k] = acc[0:T]

    def mine(s, k):
        return QF[s, k] + SR[s, k].astype(F32)

    def send_up(t, k, s):
        @pl.when(z == 0)
        def _():
            UPOUT[t, k] = mine(s, k).astype(BF16)

        @pl.when(z > 0)
        def _():
            up_in(t, k).wait_recv()
            UPOUT[t, k] = (mine(s, k) + UPIN[t, k].astype(F32)).astype(BF16)

        up_out(t, k).start()

    def send_down(t, k, s):
        @pl.when(z == ZS - 1)
        def _():
            DNOUT[t, k] = mine(s, k).astype(BF16)

        @pl.when(z < ZS - 1)
        def _():
            down_in(t, k).wait_recv()
            DNOUT[t, k] = (mine(s, k) + DNIN[t, k].astype(F32)).astype(BF16)

        down_out(t, k).start()

    def chain(t, k):
        share(t, k).wait_recv()
        if t == 0:
            @pl.when(z == 0)
            def _():
                send_up(0, k, 0)

            @pl.when(z == ZS - 1)
            def _():
                send_down(0, k, 0)
        elif t == 1:
            @pl.when(z <= 1)
            def _():
                send_up(1, k, 1)

            @pl.when(z >= 2)
            def _():
                send_down(1, k, 1)
        else:
            @pl.when(z <= 1)
            def _():
                send_up(2, k, 2)

            @pl.when(z >= 2)
            def _():
                send_down(2, k, 2)

            @pl.when(z == 1)
            def _():
                send_down(2, k, 0)

            @pl.when(z == 2)
            def _():
                send_up(2, k, 0)

    def final(k):
        share(3, k).wait_recv()
        FIN[...] = mine(3, k)

        @pl.when(z > 0)
        def _():
            t = jnp.maximum(z - 1, 0)
            up_in(t, k).wait_recv()
            FIN[...] += UPIN[t, k].astype(F32)

        @pl.when(z < ZS - 1)
        def _():
            t = jnp.maximum(2 - z, 0)
            down_in(t, k).wait_recv()
            FIN[...] += DNIN[t, k].astype(F32)

        out_ref[:, pl.ds(pl.multiple_of(k * WIDE, WIDE), WIDE)] = FIN[...].astype(BF16)

    def chunk_ready(d):
        @pl.when(z - d >= 0)
        def _():
            sib_arrival(d, z - d).wait_recv()

        @pl.when(z + d <= ZS - 1)
        def _():
            sib_arrival(3 + d, z + d).wait_recv()

    pass_on(refs_down(0, x))
    begin(over_y(refs_saved(0)))
    pass_on(refs_down(1, x))
    begin(over_y(refs_gu(0, x)))
    pass_on(refs_down(2, x))
    begin(over_y(refs_gu(1, x)))
    take_up(1)
    take_down(1)
    pass_on(refs_down(3, x))
    for copy in local:
        copy.wait()
    for o in range(1, 8):
        remote(META.at[o], META.at[o], meta_send.at[o], meta_recv.at[o], column(o)).wait_recv()
    arrive(from_y(refs_saved(0)))
    begin(over_y(refs_gu(2, x)))
    for n in range(4):
        arrive(over_x(refs_down(n, 1 - x)))
    chunk_ready(1)
    hidden(0)

    def round0(i, _):
        @pl.when(i < NK)
        def _():
            pass_on(refs_gu(i, x))

        @pl.when(i + 3 < NK)
        def _():
            begin(over_y(refs_gu(i + 3, x)))

        for s in (1, 2, 3):
            @pl.when(i == NK - 4 + s)
            def _():
                begin(over_y(refs_saved(s)))

        @pl.when(i == 2)
        def _():
            take_up(2)
            take_down(2)

        @pl.when(i >= 1)
        def _():
            arrive(over_x(refs_gu(i - 1, 1 - x)))
            compute(0, i - 1)

        @pl.when(i >= 2)
        def _():
            chain(0, i - 2)

        return 0

    lax.fori_loop(0, NK + 2 - 1, round0, 0)
    chain(0, NK - 1)
    arrive(from_y(refs_saved(1)))
    chunk_ready(2)
    hidden(1)

    def round1(i, _):
        @pl.when(i < NK)
        def _():
            compute(1, i)

        @pl.when(i >= 1)
        def _():
            chain(1, i - 1)

        @pl.when(i == 0)
        def _():
            take_up(3)
            take_down(3)

        return 0

    lax.fori_loop(0, NK + 1, round1, 0)
    arrive(from_y(refs_saved(2)))
    chunk_ready(3)
    hidden(2)
    arrive(from_y(refs_saved(3)))
    sib_arrival(0, z).wait_recv()

    def round2(i, _):
        @pl.when(i < NK)
        def _():
            compute(2, i)

        @pl.when(i >= 1)
        def _():
            chain(2, i - 1)

        @pl.when(i == 0)
        def _():
            hidden(3)

        @pl.when(i < NK)
        def _():
            compute(3, i)

        return 0

    lax.fori_loop(0, NK + 1, round2, 0)
    for o in range(1, 8):
        remote(PRS.at[(me + o) % 8], PRR.at[o], pr_send.at[o], pr_recv.at[o], column(o)).start()
    lax.fori_loop(0, NK, lambda k, _: (final(k), 0)[1], 0)

    total = PRS[me]
    for o in range(1, 8):
        remote(PRR.at[o], PRR.at[o], pr_send.at[o], pr_recv.at[o], column(o)).wait_recv()
        total = total + PRR[o]
    prod_ref[...] = total

    for o in range(1, 8):
        remote(META.at[0], META.at[o], meta_send.at[o], meta_recv.at[o], column(o)).wait_send()
        remote(PRS.at[(me + o) % 8], PRR.at[o], pr_send.at[o], pr_recv.at[o], column(o)).wait_send()
    for n in range(4):
        for copy in over_y(refs_down(n, x)) + over_x(refs_down(n, x)) + over_y(refs_saved(n)):
            copy.wait_send()
    sib_copy(0, z, x_hbm).wait_send()

    @pl.when(z < ZS - 1)
    def _():
        up_copy(0, x_hbm).wait_send()

    @pl.when(z > 0)
    def _():
        down_copy(0, x_hbm).wait_send()

    for d in range(1, ZS):
        @pl.when(z - d >= 0)
        def _():
            sib_copy(d, z - d, chunk(z - d)).wait_send()
            if d < ZS - 1:
                @pl.when(z + 1 <= ZS - 1)
                def _():
                    up_copy(d, chunk(z - d)).wait_send()

        @pl.when(z + d <= ZS - 1)
        def _():
            sib_copy(3 + d, z + d, chunk(z + d)).wait_send()
            if d < ZS - 1:
                @pl.when(z - 1 >= 0)
                def _():
                    down_copy(d, chunk(z + d)).wait_send()

    def finish(k, _):
        for copy in over_y(refs_gu(k, x)) + over_x(refs_gu(k, x)):
            copy.wait_send()
        for s in range(4):
            share(s, k).wait_send()
        for t in range(3):
            @pl.when(z <= t)
            def _():
                up_out(t, k).wait_send()

            @pl.when(z >= ZS - 1 - t)
            def _():
                down_out(t, k).wait_send()
        return 0

    lax.fori_loop(0, NK, finish, 0)


def fused_on_device(
    grad_out, expert_ids, scores, gate_weight, up_weight, down_weight, saved_gate, saved_up
):
    T, D = grad_out.shape
    H = gate_weight.shape[2]
    cap = saved_gate.shape[1] // 16
    NK = D // WIDE
    dma = pltpu.SemaphoreType.DMA
    vmem = pl.BlockSpec(memory_space=pltpu.VMEM)
    hbm = pl.BlockSpec(memory_space=pl.ANY)
    grad_in, products = pl.pallas_call(
        fused,
        out_shape=(jax.ShapeDtypeStruct((T, D), BF16), jax.ShapeDtypeStruct((8, T), F32)),
        in_specs=[vmem, vmem] + [hbm] * 6,
        out_specs=(vmem, vmem),
        scratch_shapes=[
            pltpu.VMEM((ZS, 2 * T, D), BF16),
            pltpu.VMEM((2, H, D), BF16),
            pltpu.VMEM((2, D, H), BF16),
            pltpu.VMEM((2, D, H), BF16),
            pltpu.VMEM((2, 2, ZS, cap, H), BF16),
            pltpu.VMEM((2, 2, ZS, cap, H), BF16),
            pltpu.VMEM((8, 8, T), F32),
            pltpu.VMEM((4, 2 * T, 4 * H), BF16),
            pltpu.VMEM((4, NK, T, WIDE), F32),
            pltpu.VMEM((4, NK, T, WIDE), BF16),
            pltpu.VMEM((4, NK, T, WIDE), BF16),
            pltpu.VMEM((3, NK, T, WIDE), BF16),
            pltpu.VMEM((3, NK, T, WIDE), BF16),
            pltpu.VMEM((3, NK, T, WIDE), BF16),
            pltpu.VMEM((3, NK, T, WIDE), BF16),
            pltpu.VMEM((T, WIDE), F32),
            pltpu.VMEM((8, 8, T), F32),
            pltpu.VMEM((8, 8, T), F32),
            dma((6,)),
            dma((12 + 2 * NK,)), dma((12 + 2 * NK,)),
            dma((4 + 2 * NK,)), dma((4 + 2 * NK,)),
            dma((2, 3)), dma((2, 3)),
            dma((7,)), dma((7,)),
            dma((8,)), dma((8,)),
            dma((8,)), dma((8,)),
            dma((4, NK)), dma((4, NK)),
            dma((3, NK)), dma((3, NK)),
            dma((3, NK)), dma((3, NK)),
        ],
        compiler_params=pltpu.CompilerParams(
            collective_id=0, has_side_effects=True, vmem_limit_bytes=62 * 1024 * 1024
        ),
    )(
        expert_ids, scores, grad_out, gate_weight[0], up_weight[0], down_weight[0],
        saved_gate.reshape(2, ZS, 2, cap, H), saved_up.reshape(2, ZS, 2, cap, H),
    )
    hit = expert_ids[:, :, None] == jnp.arange(8, dtype=jnp.int32)[None, None, :]
    picked = jnp.sum(jnp.where(hit, products.T[:, None, :], 0.0), axis=2)
    total = jnp.sum(scores, axis=1, keepdims=True)
    centred = picked - jnp.sum(picked * scores, axis=1, keepdims=True) / total
    grad_logit = route_scale / total * centred * scores * (1.0 - scores)
    return grad_in, grad_logit


def solution(mesh):
    in_specs = (
        P(("parts", "node", "rank"), None),
        P(("parts", "node", "rank"), None),
        P(("parts", "node", "rank"), None),
        P(("node", "rank"), None, None),
        P(("node", "rank"), None, None),
        P(("node", "rank"), None, None),
        P(("parts", "node", "rank"), None, None),
        P(("parts", "node", "rank"), None, None),
    )
    out_specs = (P(("parts", "node", "rank"), None), P(("parts", "node", "rank"), None))
    small = (mesh.shape["parts"], mesh.shape["node"], mesh.shape["rank"]) == (2, 2, 8)
    return jax.shard_map(
        fused_on_device if small else on_device, mesh=mesh, in_specs=in_specs, out_specs=out_specs, check_vma=False
    )
```

```python
import jax
import jax.numpy as jnp
from jax import lax
from jax.experimental import pallas as pl
from jax.experimental.pallas import tpu as pltpu
from jax.sharding import PartitionSpec as P

SPLIT = 4


route_scale = 2.5


def from_partner(block, axis, distance):
    count = lax.axis_size(axis)
    route = []
    for low in range(count):
        high = low | 1 << distance
        if high != low and high < count:
            route += [(low, high), (high, low)]
    return lax.ppermute(block, axis, route)


def take_half(stacked, chosen, axis_number):
    return lax.dynamic_index_in_dim(stacked, chosen, axis_number, keepdims=False)


def on_device(
    grad_out, expert_ids, scores, gate_weight, up_weight, down_weight, saved_gate, saved_up
):
    token_count, feature_width = grad_out.shape
    top_count = expert_ids.shape[1]
    source_count = lax.axis_size("node") * lax.axis_size("rank")
    expert_count = source_count // SPLIT
    hidden_width = gate_weight.shape[2]
    capacity = saved_gate.shape[1] // source_count
    quarter = capacity // SPLIT
    holder = lax.axis_index("rank") % SPLIT
    flat_ids = expert_ids.reshape(-1)
    onehot = (flat_ids[:, None] == jnp.arange(expert_count, dtype=jnp.int32)[None, :]).astype(
        jnp.int32
    )
    slot_index = jnp.sum((jnp.cumsum(onehot, axis=0) - onehot) * onehot, axis=1)
    slot_block = slot_index // quarter
    slot_within = slot_index % quarter
    repeated = jnp.repeat(grad_out, top_count, axis=0)
    empty_rows = jnp.zeros((expert_count * capacity, feature_width), jnp.bfloat16)
    location = (slot_block * expert_count + flat_ids) * quarter + slot_within
    buffered = (
        empty_rows.at[location]
        .set(repeated)
        .reshape(SPLIT, expert_count, 1, quarter, feature_width)
    )
    outgoing = jnp.broadcast_to(buffered, (SPLIT, expert_count, SPLIT, quarter, feature_width))
    outgoing = outgoing.reshape(SPLIT, source_count, quarter, feature_width)
    arrived = lax.all_to_all(outgoing, ("node", "rank"), split_axis=1, concat_axis=1, tiled=True)
    flat_rows = arrived.reshape(-1, feature_width)

    def arranged(saved):
        ordered = saved[0].reshape(source_count, SPLIT, quarter, hidden_width).transpose(1, 0, 2, 3)
        return ordered.reshape(-1, hidden_width).astype(jnp.float32)

    gate_pre = arranged(saved_gate)
    up_pre = arranged(saved_up)
    contract = (((1,), (1,)), ((), ()))
    d_hidden = lax.dot_general(
        flat_rows, down_weight[0], contract, preferred_element_type=jnp.float32
    )
    gate_sigmoid = jax.nn.sigmoid(gate_pre)
    gate_act = gate_pre * gate_sigmoid
    product_part = jnp.sum(d_hidden * gate_act * up_pre, axis=1).astype(jnp.bfloat16)
    d_gate = (d_hidden * up_pre * gate_sigmoid * (1.0 + gate_pre * (1.0 - gate_sigmoid))).astype(
        jnp.bfloat16
    )
    d_up = (d_hidden * gate_act).astype(jnp.bfloat16)
    partial_sum = lax.dot_general(
        d_gate, gate_weight[0], contract, preferred_element_type=jnp.float32
    )
    partial_sum = partial_sum + lax.dot_general(
        d_up, up_weight[0], contract, preferred_element_type=jnp.float32
    )
    partial_rows = partial_sum.astype(jnp.bfloat16).reshape(
        2, 2, source_count, quarter, feature_width
    )
    partial_products = product_part.reshape(2, 2, source_count, quarter)
    low_bit = holder % 2
    high_bit = holder // 2
    kept_rows = take_half(partial_rows, low_bit, 1)
    sent_rows = take_half(partial_rows, 1 - low_bit, 1)
    kept_products = take_half(partial_products, low_bit, 1)
    sent_products = take_half(partial_products, 1 - low_bit, 1)
    came_rows, came_products = from_partner((sent_rows, sent_products), "rank", 0)
    pair_rows = kept_rows.astype(jnp.float32) + came_rows.astype(jnp.float32)
    pair_products = kept_products.astype(jnp.float32) + came_products.astype(jnp.float32)
    kept_pair = take_half(pair_rows, high_bit, 0)
    sent_pair = take_half(pair_rows, 1 - high_bit, 0)
    kept_pair_products = take_half(pair_products, high_bit, 0)
    sent_pair_products = take_half(pair_products, 1 - high_bit, 0)
    came_pair, came_pair_products = from_partner((sent_pair, sent_pair_products), "rank", 1)
    summed_rows = (kept_pair + came_pair).astype(jnp.bfloat16)
    summed_products = (kept_pair_products + came_pair_products).astype(jnp.bfloat16)
    returned_rows, returned_products = (
        lax.all_to_all(summed_rows, ("node", "rank"), split_axis=0, concat_axis=0, tiled=True),
        lax.all_to_all(summed_products, ("node", "rank"), split_axis=0, concat_axis=0, tiled=True),
    )
    returned_rows = returned_rows.reshape(expert_count * capacity, feature_width)
    returned_products = returned_products.reshape(-1)
    gathered_at = flat_ids * capacity + slot_index
    picked = (
        returned_rows[gathered_at]
        .reshape(token_count, top_count, feature_width)
        .astype(jnp.float32)
    )
    picked_products = (
        returned_products[gathered_at].reshape(token_count, top_count).astype(jnp.float32)
    )
    score_total = jnp.sum(scores, axis=1, keepdims=True)
    weights = route_scale * scores / score_total
    grad_in = jnp.sum(weights[:, :, None] * picked, axis=1).astype(jnp.bfloat16)
    centred = (
        picked_products - jnp.sum(picked_products * scores, axis=1, keepdims=True) / score_total
    )
    grad_logit = route_scale / score_total * centred * scores * (1.0 - scores)
    return (grad_in, grad_logit)


MESH = pl.DeviceIdType.MESH
F32 = jnp.float32
BF16 = jnp.bfloat16
NT = (((1,), (1,)), ((), ()))
NN = (((1,), (0,)), ((), ()))
WIDE = 512
ZS = 4


def dot(a, b, how):
    return lax.dot_general(a, b, how, preferred_element_type=F32)


def fused(
    ids_ref, scores_ref, x_hbm, gate_hbm, up_hbm, down_hbm, sg_hbm, su_hbm,
    out_ref, prod_ref,
    X, WD, WG, WU, SG, SU, META, DGU, QF, SS, SR, UPIN, DNIN, UPOUT, DNOUT, FIN, PRS, PRR,
    loc_sem, y_send, y_recv, x_send, x_recv, ag_send, ag_recv, sib_send, sib_recv,
    meta_send, meta_recv, pr_send, pr_recv, cs_send, cs_recv, u_send, u_recv, d_send, d_recv,
):
    T, D = x_hbm.shape
    H = gate_hbm.shape[1]
    CAP = SG.shape[3]
    NK = D // WIDE
    x = lax.axis_index("parts")
    c = lax.axis_index("node")
    r = lax.axis_index("rank")
    z = r // 2
    y = r % 2
    me = z * 2 + c
    expert = c * 2 + z // 2

    sibling = (x, 1 - c, r)
    y_peer = (x, c, z * 2 + 1 - y)
    x_peer = (1 - x, c, r)
    above = (x, c, jnp.minimum(z + 1, ZS - 1) * 2 + y)
    below = (x, c, jnp.maximum(z - 1, 0) * 2 + y)

    def column(o):
        p = (me + o) % 8
        return (x, p % 2, (p // 2) * 2 + y)

    def remote(src, dst, send, recv, peer):
        return pltpu.make_async_remote_copy(
            src_ref=src, dst_ref=dst, send_sem=send, recv_sem=recv, device_id=peer, device_id_type=MESH
        )

    barrier = pltpu.get_barrier_semaphore()
    for peer in [y_peer, x_peer] + [column(o) for o in range(1, 8)]:
        pl.semaphore_signal(barrier, inc=1, device_id=peer, device_id_type=MESH)
    pl.semaphore_wait(barrier, 9)

    def chunk(zz):
        return X.at[zz, pl.ds(pl.multiple_of(c * T, T), T)]

    def chunk_other(zz):
        return X.at[zz, pl.ds(pl.multiple_of((1 - c) * T, T), T)]

    def up_copy(d, src):
        return remote(src, chunk(z - d), ag_send.at[0, d], ag_recv.at[0, d], above)

    def down_copy(d, src):
        return remote(src, chunk(z + d), ag_send.at[1, d], ag_recv.at[1, d], below)

    def up_arrival(d):
        return remote(chunk(z - d), chunk(z - d), ag_send.at[0, d - 1], ag_recv.at[0, d - 1], below)

    def down_arrival(d):
        return remote(chunk(z + d), chunk(z + d), ag_send.at[1, d - 1], ag_recv.at[1, d - 1], above)

    def sib_copy(n, zz, src):
        return remote(src, chunk(zz), sib_send.at[n], sib_recv.at[n], sibling)

    def sib_arrival(n, zz):
        return remote(chunk_other(zz), chunk_other(zz), sib_send.at[n], sib_recv.at[n], sibling)

    @pl.when(z < ZS - 1)
    def _():
        up_copy(0, x_hbm).start()

    @pl.when(z > 0)
    def _():
        down_copy(0, x_hbm).start()

    def piece(n):
        if n == 0:
            half = pl.ds(pl.multiple_of(x * (H // 2), H // 2), H // 2)
            return down_hbm.at[half], WD.at[1, half]
        if n == 1:
            return sg_hbm.at[:, :, 1 - y], SG.at[1]
        return su_hbm.at[:, :, 1 - y], SU.at[1]

    def y_copy(n):
        src, dst = piece(n)
        return remote(src, dst, y_send.at[n], y_recv.at[n], y_peer)

    def y_arrival(n):
        dst = piece(n)[1]
        return remote(dst, dst, y_send.at[n], y_recv.at[n], y_peer)

    def rows_of(k, which):
        return pl.ds(pl.multiple_of(k * WIDE + which * (WIDE // 2), WIDE // 2), WIDE // 2)

    def gu_copies(k):
        rows = rows_of(k, x)
        return [
            remote(gate_hbm.at[rows], WG.at[1, rows], y_send.at[3 + k], y_recv.at[3 + k], y_peer),
            remote(up_hbm.at[rows], WU.at[1, rows], y_send.at[3 + NK + k], y_recv.at[3 + NK + k], y_peer),
        ]

    def gu_arrivals(k):
        rows = rows_of(k, x)
        return [
            remote(WG.at[1, rows], WG.at[1, rows], y_send.at[3 + k], y_recv.at[3 + k], y_peer),
            remote(WU.at[1, rows], WU.at[1, rows], y_send.at[3 + NK + k], y_recv.at[3 + NK + k], y_peer),
        ]

    def gu_across(k, which):
        rows = rows_of(k, which)
        return [
            remote(WG.at[1, rows], WG.at[1, rows], x_send.at[1 + k], x_recv.at[1 + k], x_peer),
            remote(WU.at[1, rows], WU.at[1, rows], x_send.at[1 + NK + k], x_recv.at[1 + NK + k], x_peer),
        ]

    def down_across(which):
        half = pl.ds(pl.multiple_of(which * (H // 2), H // 2), H // 2)
        return remote(WD.at[1, half], WD.at[1, half], x_send.at[0], x_recv.at[0], x_peer)

    for n in range(3):
        y_copy(n).start()

    def start_gu(k, _):
        for copy in gu_copies(k):
            copy.start()
        return 0

    lax.fori_loop(0, NK, start_gu, 0)

    sib_copy(0, z, x_hbm).start()
    local = [
        pltpu.make_async_copy(x_hbm, chunk(z), loc_sem.at[0]),
        pltpu.make_async_copy(down_hbm, WD.at[0], loc_sem.at[1]),
        pltpu.make_async_copy(gate_hbm, WG.at[0], loc_sem.at[2]),
        pltpu.make_async_copy(up_hbm, WU.at[0], loc_sem.at[3]),
        pltpu.make_async_copy(sg_hbm.at[:, :, y], SG.at[0], loc_sem.at[4]),
        pltpu.make_async_copy(su_hbm.at[:, :, y], SU.at[0], loc_sem.at[5]),
    ]
    for copy in local:
        copy.start()

    lane = lax.broadcasted_iota(jnp.int32, (T, T), 1)
    row = lax.broadcasted_iota(jnp.int32, (T, T), 0)
    ids = ids_ref[...]
    scores = scores_ref[...]
    hit0 = lane == ids[:, 0:1]
    hit1 = lane == ids[:, 1:2]
    hits = jnp.where(hit0 | hit1, 1.0, 0.0)
    earlier = jnp.where(lane < row, 1.0, 0.0).astype(BF16)
    slots = jnp.where(hits > 0.5, dot(earlier, hits.astype(BF16), NN), -1.0)
    factor = route_scale / (scores[:, 0:1] + scores[:, 1:2])
    weights = jnp.where(lane == ids[:, 0:1] + 4, factor * scores[:, 0:1], 0.0)
    weights = jnp.where(lane == ids[:, 1:2] + 4, factor * scores[:, 1:2], weights)
    META[0] = jnp.transpose(jnp.where(lane < 4, slots, weights))[0:8]
    for o in range(1, 8):
        remote(META.at[0], META.at[o], meta_send.at[o], meta_recv.at[o], column(o)).start()

    def take_up(d):
        @pl.when(z - d >= 0)
        def _():
            up_arrival(d).wait_recv()
            if d < ZS - 1:
                @pl.when(z + 1 <= ZS - 1)
                def _():
                    up_copy(d, chunk(z - d)).start()
            sib_copy(d, z - d, chunk(z - d)).start()

    def take_down(d):
        @pl.when(z + d <= ZS - 1)
        def _():
            down_arrival(d).wait_recv()
            if d < ZS - 1:
                @pl.when(z - 1 >= 0)
                def _():
                    down_copy(d, chunk(z + d)).start()
            sib_copy(3 + d, z + d, chunk(z + d)).start()

    def pass_gu(k):
        for copy in gu_arrivals(k):
            copy.wait_recv()
        for copy in gu_across(k, x):
            copy.start()

    take_up(1)
    take_down(1)
    y_arrival(0).wait_recv()
    down_across(x).start()
    take_up(2)
    take_down(2)
    ready = 4
    for copy in local:
        copy.wait()
    y_arrival(1).wait_recv()
    y_arrival(2).wait_recv()
    down_across(1 - x).wait_recv()
    for o in range(1, 8):
        remote(META.at[o], META.at[o], meta_send.at[o], meta_recv.at[o], column(o)).wait_recv()
    sib_arrival(0, z).wait_recv()

    def chunk_ready(d):
        @pl.when(z - d >= 0)
        def _():
            sib_arrival(d, z - d).wait_recv()

        @pl.when(z + d <= ZS - 1)
        def _():
            sib_arrival(3 + d, z + d).wait_recv()

    def job(s):
        order = ((0, 1, 2, 3), (1, 0, 2, 3), (2, 3, 1, 0), (3, 2, 1, 0))
        return jnp.where(
            z == 0, order[0][s], jnp.where(z == 1, order[1][s], jnp.where(z == 2, order[2][s], order[3][s]))
        )

    slot_lane = lax.broadcasted_iota(jnp.int32, (T, CAP), 1).astype(F32)
    row8 = lax.broadcasted_iota(jnp.int32, (8, T), 0)
    ones = jnp.ones((8, H), BF16)

    def hidden(zz, _):
        hs = [dot(X[zz], WD[b], NT) for b in range(2)]
        for cc in range(2):
            o = (me - (zz * 2 + cc) + 8) % 8
            meta = jnp.transpose(jnp.concatenate([META[o], jnp.zeros((T - 8, T), F32)], axis=0))
            slot = jnp.sum(jnp.where(lane == expert, meta, 0.0), axis=1, keepdims=True)
            weight = jnp.sum(jnp.where(lane == expert + 4, meta, 0.0), axis=1, keepdims=True)
            pick = jnp.where(slot == slot_lane, 1.0, 0.0).astype(BF16)
            total = jnp.zeros((8, T), F32)
            for b in range(2):
                h = hs[b][cc * T:(cc + 1) * T]
                g = dot(pick, SG[b, cc, zz], NN)
                u = dot(pick, SU[b, cc, zz], NN)
                sig = jax.nn.sigmoid(g)
                act = g * sig
                prod = h * act * u
                high = prod.astype(BF16)
                low = (prod - high.astype(F32)).astype(BF16)
                total = total + dot(ones, high, NT) + dot(ones, low, NT)
                scaled = h * weight
                rows = pl.ds(pl.multiple_of(zz * T, T), T)
                DGU[cc, rows, b * 2 * H:b * 2 * H + H] = (
                    scaled * u * sig * (1.0 + g * (1.0 - sig))
                ).astype(BF16)
                DGU[cc, rows, b * 2 * H + H:(b + 1) * 2 * H] = (scaled * act).astype(BF16)
            PRS[zz * 2 + cc] = jnp.where(row8 == expert, total, 0.0)
        return 0

    hidden(job(0), 0)
    chunk_ready(1)
    pass_gu(0)
    hidden(job(1), 0)
    chunk_ready(2)
    pass_gu(1)
    hidden(job(2), 0)
    pass_gu(2)
    pass_gu(3)
    take_up(3)
    take_down(3)
    chunk_ready(3)
    hidden(job(3), 0)
    for o in range(1, 8):
        remote(PRS.at[(me + o) % 8], PRR.at[o], pr_send.at[o], pr_recv.at[o], column(o)).start()

    def share(k):
        return remote(SS.at[k], SR.at[k], cs_send.at[k], cs_recv.at[k], sibling)

    def up_out(k, d):
        return remote(UPOUT.at[d - 1, k], UPIN.at[d - 1, k], u_send.at[d - 1, k], u_recv.at[d - 1, k], above)

    def down_out(k, d):
        return remote(DNOUT.at[d - 1, k], DNIN.at[d - 1, k], d_send.at[d - 1, k], d_recv.at[d - 1, k], below)

    def up_in(k, d):
        return remote(UPIN.at[d, k], UPIN.at[d, k], u_send.at[d, k], u_recv.at[d, k], below)

    def down_in(k, d):
        return remote(DNIN.at[d, k], DNIN.at[d, k], d_send.at[d, k], d_recv.at[d, k], above)

    def partial(k, cc):
        rows = pl.ds(pl.multiple_of(k * WIDE, WIDE), WIDE)
        acc = dot(DGU[cc, :, 0:H], WG[0, rows], NT)
        acc = acc + dot(DGU[cc, :, H:2 * H], WU[0, rows], NT)
        acc = acc + dot(DGU[cc, :, 2 * H:3 * H], WG[1, rows], NT)
        return acc + dot(DGU[cc, :, 3 * H:4 * H], WU[1, rows], NT)

    def compute(k):
        for copy in gu_across(k, 1 - x):
            copy.wait_recv()
        SS[k] = partial(k, 1 - c).reshape(ZS, T, WIDE).astype(BF16)
        share(k).start()
        QF[k % 4] = partial(k, c).reshape(ZS, T, WIDE)

    def mine(k, zz):
        return QF[k % 4, zz] + SR[k, zz].astype(F32)

    def chain(k):
        share(k).wait_recv()
        for d in (3, 2, 1):
            @pl.when(z + d <= ZS - 1)
            def _():
                @pl.when(z == 0)
                def _():
                    UPOUT[d - 1, k] = mine(k, z + d).astype(BF16)
                if d < 3:
                    @pl.when(z > 0)
                    def _():
                        up_in(k, d).wait_recv()
                        UPOUT[d - 1, k] = (mine(k, z + d) + UPIN[d, k].astype(F32)).astype(BF16)
                up_out(k, d).start()

            @pl.when(z - d >= 0)
            def _():
                @pl.when(z == ZS - 1)
                def _():
                    DNOUT[d - 1, k] = mine(k, z - d).astype(BF16)
                if d < 3:
                    @pl.when(z < ZS - 1)
                    def _():
                        down_in(k, d).wait_recv()
                        DNOUT[d - 1, k] = (mine(k, z - d) + DNIN[d, k].astype(F32)).astype(BF16)
                down_out(k, d).start()

    def final(k):
        FIN[...] = mine(k, z)

        @pl.when(z > 0)
        def _():
            up_in(k, 0).wait_recv()
            FIN[...] += UPIN[0, k].astype(F32)

        @pl.when(z < ZS - 1)
        def _():
            down_in(k, 0).wait_recv()
            FIN[...] += DNIN[0, k].astype(F32)

        out_ref[:, pl.ds(pl.multiple_of(k * WIDE, WIDE), WIDE)] = FIN[...].astype(BF16)

    def step(i, _):
        @pl.when(i + ready < NK)
        def _():
            pass_gu(i + ready)

        @pl.when(i < NK)
        def _():
            compute(i)

        @pl.when((i >= 1) & (i <= NK))
        def _():
            chain(i - 1)

        @pl.when(i >= 2)
        def _():
            final(i - 2)

        return 0

    lax.fori_loop(0, NK + 2, step, 0)

    total = PRS[me]
    for o in range(1, 8):
        remote(PRR.at[o], PRR.at[o], pr_send.at[o], pr_recv.at[o], column(o)).wait_recv()
        total = total + PRR[o]
    prod_ref[...] = total

    for o in range(1, 8):
        remote(META.at[0], META.at[o], meta_send.at[o], meta_recv.at[o], column(o)).wait_send()
        remote(PRS.at[(me + o) % 8], PRR.at[o], pr_send.at[o], pr_recv.at[o], column(o)).wait_send()
    for n in range(3):
        y_copy(n).wait_send()
    down_across(x).wait_send()
    sib_copy(0, z, x_hbm).wait_send()

    @pl.when(z < ZS - 1)
    def _():
        up_copy(0, x_hbm).wait_send()

    @pl.when(z > 0)
    def _():
        down_copy(0, x_hbm).wait_send()

    for d in range(1, ZS):
        @pl.when(z - d >= 0)
        def _():
            sib_copy(d, z - d, chunk(z - d)).wait_send()
            if d < ZS - 1:
                @pl.when(z + 1 <= ZS - 1)
                def _():
                    up_copy(d, chunk(z - d)).wait_send()

        @pl.when(z + d <= ZS - 1)
        def _():
            sib_copy(3 + d, z + d, chunk(z + d)).wait_send()
            if d < ZS - 1:
                @pl.when(z - 1 >= 0)
                def _():
                    down_copy(d, chunk(z + d)).wait_send()

    def finish(k, _):
        for copy in gu_copies(k) + gu_across(k, x):
            copy.wait_send()
        share(k).wait_send()
        for d in (3, 2, 1):
            @pl.when(z + d <= ZS - 1)
            def _():
                up_out(k, d).wait_send()

            @pl.when(z - d >= 0)
            def _():
                down_out(k, d).wait_send()
        return 0

    lax.fori_loop(0, NK, finish, 0)


def fused_on_device(
    grad_out, expert_ids, scores, gate_weight, up_weight, down_weight, saved_gate, saved_up
):
    T, D = grad_out.shape
    H = gate_weight.shape[2]
    cap = saved_gate.shape[1] // 16
    NK = D // WIDE
    dma = pltpu.SemaphoreType.DMA
    vmem = pl.BlockSpec(memory_space=pltpu.VMEM)
    hbm = pl.BlockSpec(memory_space=pl.ANY)
    grad_in, products = pl.pallas_call(
        fused,
        out_shape=(jax.ShapeDtypeStruct((T, D), BF16), jax.ShapeDtypeStruct((8, T), F32)),
        in_specs=[vmem, vmem] + [hbm] * 6,
        out_specs=(vmem, vmem),
        scratch_shapes=[
            pltpu.VMEM((ZS, 2 * T, D), BF16),
            pltpu.VMEM((2, H, D), BF16),
            pltpu.VMEM((2, D, H), BF16),
            pltpu.VMEM((2, D, H), BF16),
            pltpu.VMEM((2, 2, ZS, cap, H), BF16),
            pltpu.VMEM((2, 2, ZS, cap, H), BF16),
            pltpu.VMEM((8, 8, T), F32),
            pltpu.VMEM((2, ZS * T, 4 * H), BF16),
            pltpu.VMEM((4, ZS, T, WIDE), F32),
            pltpu.VMEM((NK, ZS, T, WIDE), BF16),
            pltpu.VMEM((NK, ZS, T, WIDE), BF16),
            pltpu.VMEM((3, NK, T, WIDE), BF16),
            pltpu.VMEM((3, NK, T, WIDE), BF16),
            pltpu.VMEM((3, NK, T, WIDE), BF16),
            pltpu.VMEM((3, NK, T, WIDE), BF16),
            pltpu.VMEM((T, WIDE), F32),
            pltpu.VMEM((8, 8, T), F32),
            pltpu.VMEM((8, 8, T), F32),
            dma((6,)),
            dma((3 + 2 * NK,)), dma((3 + 2 * NK,)),
            dma((1 + 2 * NK,)), dma((1 + 2 * NK,)),
            dma((2, 3)), dma((2, 3)),
            dma((7,)), dma((7,)),
            dma((8,)), dma((8,)),
            dma((8,)), dma((8,)),
            dma((NK,)), dma((NK,)),
            dma((3, NK)), dma((3, NK)),
            dma((3, NK)), dma((3, NK)),
        ],
        compiler_params=pltpu.CompilerParams(
            collective_id=0, has_side_effects=True, vmem_limit_bytes=62 * 1024 * 1024
        ),
    )(
        expert_ids, scores, grad_out, gate_weight[0], up_weight[0], down_weight[0],
        saved_gate.reshape(2, ZS, 2, cap, H), saved_up.reshape(2, ZS, 2, cap, H),
    )
    hit = expert_ids[:, :, None] == jnp.arange(8, dtype=jnp.int32)[None, None, :]
    picked = jnp.sum(jnp.where(hit, products.T[:, None, :], 0.0), axis=2)
    total = jnp.sum(scores, axis=1, keepdims=True)
    centred = picked - jnp.sum(picked * scores, axis=1, keepdims=True) / total
    grad_logit = route_scale / total * centred * scores * (1.0 - scores)
    return grad_in, grad_logit


def solution(mesh):
    in_specs = (
        P(("parts", "node", "rank"), None),
        P(("parts", "node", "rank"), None),
        P(("parts", "node", "rank"), None),
        P(("node", "rank"), None, None),
        P(("node", "rank"), None, None),
        P(("node", "rank"), None, None),
        P(("parts", "node", "rank"), None, None),
        P(("parts", "node", "rank"), None, None),
    )
    out_specs = (P(("parts", "node", "rank"), None), P(("parts", "node", "rank"), None))
    small = (mesh.shape["parts"], mesh.shape["node"], mesh.shape["rank"]) == (2, 2, 8)
    return jax.shard_map(
        fused_on_device if small else on_device, mesh=mesh, in_specs=in_specs, out_specs=out_specs, check_vma=False
    )
```
